1024 devices in a mesh: dp: 16 (over y, core), emb: 64 (over x, z).
Axes of the slice: x: 4, y: 8, z: 16, core: 2. Of those that a mesh axis runs over, the one named last changes fastest.
Arguments:
- table: bfloat16 [32768, 512], P('emb'), may hold values from -6 to 6
- item_shard: int32 [262144, 1], P(('dp', 'emb')), may hold values from 0 to 63; in each aligned block of 256 rows (0 to 255, 256 to 511, ...) at most 8 rows name the same one
- item_row: int32 [262144], P(('dp', 'emb')), may hold values from 0 to 511
- segment_ids: int32 [1024, 256], P(('dp', 'emb')), may hold values from 0 to 15, never falling along the last dimension, each value on 1 to 128 neighbouring positions
- grad_out: bfloat16 [262144, 512], P(('dp', 'emb')), may hold values from -6 to 6
- w_in: bfloat16 [512, 2048], replicated, may hold values from -0.25 to 0.25
- w_out: bfloat16 [512, 512], replicated, may hold values from -0.25 to 0.25
Outputs:
- mixed: bfloat16 [262144, 512], P(('dp', 'emb'))
- table_grad: float32 [32768, 512], P(('emb', 'dp'))
The draws below stay inside these ranges and needn't reach their ends.
Inputs may be any that keep to these rules, and one draw needn't show every extreme that they name: `item_shard`: at most 8 tokens of one device name one table shard; in every draw some device has exactly 8 tokens for some shard. `segment_ids`: within each row never falling; each of the 16 histories has 1 to 128 tokens, one exactly 128.
All inputs are finite; a program needn't handle non-finite values.
Results may differ from the reference program's by a relative error of at most 0.022.
Values may be sent and summed in bfloat16 or wider, within the bound.
A program may use at most 32 MiB of HBM per device.

```python
import math
import jax
import jax.numpy as jnp
import numpy as np
from jax import lax

D = 512
HEADS = 8
TOK_DEV = 256
ROWS_DEV = 512
CAP = 8
MOST = 128
HISTS = 16
TOKENS = 262144
ITEMS = 32768
N_EMB = 64
DEVICES = 1024


def plant(drawn, stream_key, least, top_value):
    shape = drawn.shape
    spot = [jax.random.randint(jax.random.fold_in(stream_key, axis), (), 0, shape[axis]) for axis in range(len(shape))]
    drawn = drawn.at[tuple(spot)].set(least)
    longest = shape.index(max(shape))
    spot[longest] = (spot[longest] + 1) % shape[longest]
    return drawn.at[tuple(spot)].set(top_value)


def block_levels(key, shape, shards, low, high):
    gain = 1.0
    for axis_at, parts in shards:
        heights = jax.random.uniform(jax.random.fold_in(jax.random.fold_in(key, 6), axis_at), (parts,), jnp.float32, low / len(shards), high / len(shards))
        gain = gain * jnp.repeat(jnp.exp(heights), shape[axis_at] // parts).reshape((-1,) + (1,) * (len(shape) - 1 - axis_at))
    return gain


def profile(amount, total, bound, slope):
    weights = [(1 << 20) // math.isqrt(standing ** slope) + 1 for standing in range(2, amount + 1)]
    surplus, given = total - bound - (amount - 1), [1] * (amount - 1)
    while surplus > 0:
        movable = [i for i in range(amount - 1) if given[i] < bound]
        whole, budget = sum([weights[i] for i in movable]), surplus
        for i in movable:
            addition = min(bound - given[i], max(1, budget * weights[i] // whole), surplus)
            given[i] = given[i] + addition
            surplus = surplus - addition
    return np.array([bound] + given)


def uneven(own_key, amount, total, limit, lean):
    if amount == 2:
        one = jax.random.randint(own_key, (), max(1, total - limit), min(limit, total - 1) + 1)
        return jnp.stack([one, total - one])
    tallies = jnp.asarray(profile(amount, total, limit, lean), jnp.int32)
    couples = (amount - 1) // 2
    giver, sink = tallies[1:1 + 2 * couples:2], tallies[2:2 + 2 * couples:2]
    margin = jnp.minimum(giver - 1, limit - sink)
    passed = jax.random.randint(jax.random.fold_in(own_key, 1), (couples,), 0, 1 << 20) % (margin + 1)
    tallies = tallies.at[1:1 + 2 * couples:2].set(giver - passed).at[2:2 + 2 * couples:2].set(sink + passed)
    return tallies[jax.random.permutation(jax.random.fold_in(own_key, 2), amount)]


def assign_block(own_key, own, number, rows, amount, top, reach, lean):
    ranking = jax.random.permutation(own_key, amount)
    crowded, common = load_shares(amount, rows * top, reach, lean, True), load_shares(amount, rows * top, reach, lean, False)
    places = jnp.arange(amount)

    def named(sizes, turn):
        used = int((sizes > 0).sum())
        fixed = max(1, used // 4)
        passed = fixed + (places - fixed + turn * (used - fixed)) % max(1, amount - fixed)
        return jnp.zeros((amount,), jnp.int32).at[ranking[jnp.where(places < fixed, places, passed)]].set(jnp.asarray(sizes, jnp.int32))

    sizes = jnp.where(number % 4 == 0, named(crowded, number // 4), named(common, number - number // 4 - 1))
    mixed = jax.random.permutation(jax.random.fold_in(own, 3), amount)
    giver, sink = mixed[0:amount // 2 * 2:2], mixed[1:amount // 2 * 2:2]
    slack = jnp.minimum(sizes[giver] - 1, reach - sizes[sink]) // 2
    slack = jnp.where((giver == ranking[0]) | (sink == ranking[0]) | (sizes[sink] == 0), 0, jnp.maximum(slack, 0))
    passed = jax.random.randint(jax.random.fold_in(own, 4), (amount // 2,), 0, 1 << 20) % (slack + 1)
    sizes = sizes.at[giver].add(-passed).at[sink].add(passed)
    members = jnp.searchsorted(jnp.cumsum(sizes), jnp.arange(rows * top), side="right").astype(jnp.int32)
    table = members.reshape(top, rows).T
    table = table[jax.random.permutation(jax.random.fold_in(own, 1), rows)]
    turn = jax.random.randint(jax.random.fold_in(own, 2), (rows, 1), 0, top)
    return jnp.take_along_axis(table, (jnp.arange(top)[None, :] + turn) % top, axis=1)


def load_shares(count, total, bound, skew, full):
    portions = [(1 << 20) // math.isqrt(standing ** skew) + 1 for standing in range(1, count + 1)]
    largest = bound if full else min(bound, max(-(-total // count), total * portions[0] // sum(portions)))
    least = 1 if total - largest >= count - 1 else 0
    counts, spare = [largest] + [least] * (count - 1), total - largest - least * (count - 1)
    while spare > 0:
        free = [i for i in range(1, count) if counts[i] < largest] or [i for i in range(1, count) if counts[i] < bound]
        pool, left = sum([portions[i] for i in free]), spare
        for i in free:
            addition = min(bound - counts[i], max(1, left * portions[i] // pool), spare)
            counts[i] = counts[i] + addition
            spare = spare - addition
    return np.array(counts)


def noise(key, shape, scale, most, shards=(), dtype=jnp.bfloat16):
    array = scale * jax.random.normal(key, shape, jnp.float32)
    if shards:
        array = array * block_levels(key, shape, shards, -0.22, 0.18)
    return jnp.clip(array, -most, most).astype(dtype)


def setup_inputs(seed: int = 0) -> dict:
    streams_of = jax.random.split(jax.random.key(seed), 8)
    table = noise(streams_of[0], (ITEMS, D), 1.0, 6.0, ((0, 64),))
    item_shard_keys = jax.random.split(jax.random.fold_in(streams_of[1], 1), TOKENS // TOK_DEV)
    item_shard_turns = jax.random.permutation(jax.random.fold_in(streams_of[1], 3), TOKENS // TOK_DEV)
    item_shard = jax.vmap(lambda own, number: assign_block(jax.random.fold_in(streams_of[1], 2), own, number, TOK_DEV, N_EMB, 1, CAP, 2))(item_shard_keys, item_shard_turns).reshape((TOKENS, 1))
    item_row = plant(jax.random.randint(streams_of[2], (TOKENS,), 0, ROWS_DEV), jax.random.fold_in(streams_of[2], 1), 0, ROWS_DEV - 1).astype(jnp.int32)
    segment_ids = jax.vmap(lambda own: jnp.searchsorted(jnp.cumsum(uneven(own, HISTS, TOK_DEV, MOST, 2)), jnp.arange(TOK_DEV), side="right"))(jax.random.split(streams_of[3], DEVICES)).reshape((DEVICES, TOK_DEV)).astype(jnp.int32)
    grad_out = noise(streams_of[4], (TOKENS, D), 1.0, 6.0, ((0, 1024),))
    w_in = noise(streams_of[5], (D, 4 * D), D ** -0.5, 0.25)
    w_out = noise(streams_of[6], (D, D), D ** -0.5, 0.25)
    return dict(table=table, item_shard=item_shard, item_row=item_row, segment_ids=segment_ids, grad_out=grad_out, w_in=w_in, w_out=w_out)


def layer(x, seg, w_in, w_out):
    length, width = x.shape
    proj = jax.nn.silu(jnp.dot(x, w_in, preferred_element_type=jnp.float32)).astype(jnp.bfloat16)
    u_part, v_part, q_part, k_part = jnp.split(proj, 4, axis=1)
    queries = q_part.reshape(length, HEADS, -1)
    keys_all = k_part.reshape(length, HEADS, -1)
    values = v_part.reshape(length, HEADS, -1)
    scores = jnp.einsum('qhd,khd->hqk', queries, keys_all, preferred_element_type=jnp.float32) * queries.shape[2] ** (-0.5)
    place = jnp.arange(length)
    causal = (place[None, :] <= place[:, None]) & (seg[:, None] == seg[None, :])
    weights = jnp.where(causal[None], jax.nn.silu(scores) / MOST, 0.0).astype(jnp.bfloat16)
    attended = jnp.einsum('hqk,khd->qhd', weights, values, preferred_element_type=jnp.float32).reshape(length, width)
    center = attended - lax.optimization_barrier(jnp.mean(attended, axis=1, keepdims=True))
    normed = center * lax.rsqrt(lax.optimization_barrier(jnp.mean(center * center, axis=1, keepdims=True)) + 1e-05)
    gated = (normed * u_part.astype(jnp.float32)).astype(jnp.bfloat16)
    return (jnp.dot(gated, w_out, preferred_element_type=jnp.float32) + x.astype(jnp.float32)).astype(jnp.bfloat16)

def reference(table, item_shard, item_row, segment_ids, grad_out, w_in, w_out):
    item = (item_shard[:, 0] * ROWS_DEV + item_row).astype(jnp.int32)
    embedded = table[item]
    blocks = embedded.reshape(DEVICES, TOK_DEV, D)
    cotangents = grad_out.reshape(DEVICES, TOK_DEV, D)

    def one_block(packed):
        block, seg, cotangent = packed
        output, pull = jax.vjp(lambda inputs: layer(inputs, seg, w_in, w_out), block)
        d_block, = pull(cotangent)
        return (output, d_block)
    mixed, d_embedded = lax.map(one_block, (blocks, segment_ids, cotangents))
    table_grad = jnp.zeros((ITEMS, D), jnp.float32).at[item].add(d_embedded.reshape(TOKENS, D).astype(jnp.float32))
    return (mixed.reshape(TOKENS, D), table_grad)
```

```python
import functools

import jax
import jax.numpy as jnp
from jax import lax
from jax.experimental import pallas as pl
from jax.experimental.pallas import tpu as pltpu
from jax.sharding import PartitionSpec as P

HEADS = 8
CAP = 8
MOST = 128
MESH = pl.DeviceIdType.MESH
F32 = jnp.float32
BF16 = jnp.bfloat16


def dot(a, b, contract=(1, 0)):
    return lax.dot_general(
        a, b, (((contract[0],), (contract[1],)), ((), ())), preferred_element_type=F32
    )


def iota(shape, axis):
    return lax.broadcasted_iota(jnp.int32, shape, axis)


def to_col(row):
    n = row.shape[1]
    return jnp.sum(jnp.where(iota((n, n), 0) == iota((n, n), 1), row, 0.0), axis=1, keepdims=True)


def sigmoid(value):
    return 0.5 * jnp.tanh(0.5 * value) + 0.5


def near(step, size):
    return jnp.where(step % 2 == 1, (step + 1) // 2, size - step // 2)


def forward_backward(seg_row, x_ref, grad_ref, win_ref, wout_ref, mixed_ref, dx_ref,
                     proj_ref, slope_ref, weight_ref, wslope_ref, dz_ref):
    tokens, width = x_ref.shape
    pairs = HEADS // 2
    lanes = 2 * width // HEADS
    scale = (width // HEADS) ** -0.5

    def part(index):
        return slice(index * width, (index + 1) * width)

    x = x_ref[...]
    for index in range(4):
        z = dot(x, win_ref[:, part(index)])
        sig = sigmoid(z)
        act = z * sig
        proj_ref[:, part(index)] = act.astype(BF16)
        slope_ref[:, part(index)] = sig + act * (1.0 - sig)

    seg_col = to_col(seg_row)
    seen = (iota((tokens, tokens), 1) <= iota((tokens, tokens), 0)) & (seg_col == seg_row)
    factor = jnp.where(seen, 1.0 / MOST, 0.0)
    factor = jnp.concatenate([factor, factor], axis=0)
    first = iota((tokens, lanes), 1) < lanes // 2

    def stack(value):
        zero = jnp.zeros_like(value)
        return jnp.concatenate([jnp.where(first, value, zero), jnp.where(first, zero, value)], axis=0)

    def unstack(value):
        return jnp.where(first, value[:tokens], value[tokens:])

    def pair(index, which):
        start = which * width + index * lanes
        return slice(start, start + lanes)

    attended = []
    for index in range(pairs):
        q = stack(proj_ref[:, pair(index, 2)])
        s = dot(q, proj_ref[:, pair(index, 3)], (1, 1)) * scale
        sig = sigmoid(s)
        act = s * sig
        weights = (act * factor).astype(BF16)
        weight_ref[index] = weights
        wslope_ref[index] = (sig + act * (1.0 - sig)) * (factor * scale)
        attended.append(unstack(dot(weights, proj_ref[:, pair(index, 1)])))
    attended = jnp.concatenate(attended, axis=1)

    center = attended - jnp.mean(attended, axis=1, keepdims=True)
    rstd = lax.rsqrt(jnp.mean(center * center, axis=1, keepdims=True) + 1e-05)
    normed = center * rstd
    u = proj_ref[:, part(0)].astype(F32)
    gated = (normed * u).astype(BF16)
    mixed_ref[...] = (dot(gated, wout_ref[...]) + x.astype(F32)).astype(BF16)

    d_gated = dot(grad_ref[...], wout_ref[...], (1, 1)).astype(BF16).astype(F32)
    d_u = (d_gated * normed).astype(BF16).astype(F32)
    dz_ref[:, part(0)] = (d_u * slope_ref[:, part(0)]).astype(BF16)
    d_normed = d_gated * u
    d_att = rstd * (
        d_normed
        - jnp.mean(d_normed, axis=1, keepdims=True)
        - normed * jnp.mean(d_normed * normed, axis=1, keepdims=True)
    )
    d_att = d_att.astype(BF16)

    def put(index, which, value):
        value = value.astype(BF16).astype(F32)
        dz_ref[:, pair(index, which)] = (value * slope_ref[:, pair(index, which)]).astype(BF16)

    for index in range(pairs):
        q = stack(proj_ref[:, pair(index, 2)])
        d = stack(d_att[:, index * lanes:(index + 1) * lanes])
        put(index, 1, dot(weight_ref[index], d, (0, 0)))
        d_s = dot(d, proj_ref[:, pair(index, 1)], (1, 1)) * wslope_ref[index]
        d_s = d_s.astype(BF16)
        put(index, 2, unstack(dot(d_s, proj_ref[:, pair(index, 3)])))
        put(index, 3, dot(d_s, q, (0, 0)))

    d_x = dot(dz_ref[...], win_ref[...], (1, 1)).astype(BF16).astype(F32)
    dx_ref[...] = (d_x + grad_ref[...].astype(F32)).astype(BF16)


def kernel(nx, nz, nd, chunks,
           owner_ref, row_ref, seg_ref, table_hbm, grad_hbm, win_hbm, wout_hbm,
           mixed_ref, out_ref,
           table_ref, grad_ref, win_ref, wout_ref,
           ask_ref, mid_ref, comb_ref, fin_ref,
           place_ref, back_ref, put_ref,
           send_ref, recv_ref, x_ref, dx_ref,
           proj_ref, slope_ref, weight_ref, wslope_ref, dz_ref,
           gsend_ref, grecv_ref, dsend_ref, drecv_ref,
           load_sem, zs_sem, zr_sem, xs_sem, xr_sem, rs_sem, rr_sem, gs_sem, gr_sem, ds_sem, dr_sem):
    emb = lax.axis_index("emb")
    dp = lax.axis_index("dp")
    x_at, z_at = emb // nz, emb % nz
    groups = nx * nz
    tokens, width = x_ref.shape
    rows = table_ref.shape[0]
    lanes = nz * CAP
    half = width // (2 * chunks)

    loads = [
        pltpu.make_async_copy(source, target, load_sem.at[index])
        for index, (source, target) in enumerate(
            [(table_hbm, table_ref), (win_hbm, win_ref), (wout_hbm, wout_ref), (grad_hbm, grad_ref)]
        )
    ]
    for load in loads:
        load.start()

    barrier = pltpu.get_barrier_semaphore()

    def greet(step, carry):
        pl.semaphore_signal(barrier, 1, device_id={"emb": (emb + step) % groups}, device_id_type=MESH)
        return carry

    def greet_dp(step, carry):
        pl.semaphore_signal(barrier, 1, device_id={"dp": (dp + step) % nd}, device_id_type=MESH)
        return carry

    lax.fori_loop(1, groups, greet, 0)
    lax.fori_loop(1, nd, greet_dp, 0)

    def finish(ref, count, sem):
        pltpu.make_async_copy(ref.at[pl.ds(0, count)], ref.at[pl.ds(0, count)], sem).wait()

    owner = owner_ref[...].astype(F32)
    named = iota((groups, tokens), 0).astype(F32) == owner
    before = (iota((tokens, tokens), 0) < iota((tokens, tokens), 1)).astype(BF16)
    named_bf = named.astype(BF16)
    slot = jnp.sum(jnp.where(named, dot(named_bf, before), 0.0), axis=0, keepdims=True)
    target = owner * CAP + slot
    place_ref[...] = (to_col(target) == iota((tokens, groups * CAP), 1).astype(F32)).astype(BF16)
    back_ref[...] = (iota((groups * CAP, tokens), 0).astype(F32) == target).astype(BF16)
    number = to_col((row_ref[...] + 1).astype(F32))
    lane = to_col(slot) + (z_at * CAP).astype(F32)
    here = lane == iota((tokens, lanes), 1).astype(F32)
    high = jnp.floor(number * (1.0 / 16.0))
    low = number - 16.0 * high
    ask = 16.0 * dot(named_bf, jnp.where(here, high, 0.0).astype(BF16)) + dot(
        named_bf, jnp.where(here, low, 0.0).astype(BF16)
    )
    for at in range(nx):
        ask_ref[:, pl.ds(at, 1), :] = ask[at * nz:(at + 1) * nz].reshape(nz, 1, lanes)

    pl.semaphore_wait(barrier, groups + nd - 2)

    def ask_z(step, carry):
        peer = (z_at + near(step, nz)) % nz
        pltpu.make_async_remote_copy(
            src_ref=ask_ref.at[peer], dst_ref=mid_ref.at[z_at], send_sem=zs_sem, recv_sem=zr_sem,
            device_id={"emb": x_at * nz + peer}, device_id_type=MESH,
        ).start()
        return carry

    lax.fori_loop(1, nz, ask_z, 0)
    mid_ref[z_at] = ask_ref[z_at]
    finish(mid_ref, nz - 1, zr_sem)
    comb = jnp.sum(mid_ref[...], axis=0)
    for at in range(nx):
        comb_ref[at] = comb[at:at + 1]

    def ask_x(step, carry):
        peer = (x_at + step) % nx
        pltpu.make_async_remote_copy(
            src_ref=comb_ref.at[peer], dst_ref=fin_ref.at[x_at], send_sem=xs_sem, recv_sem=xr_sem,
            device_id={"emb": peer * nz + z_at}, device_id_type=MESH,
        ).start()
        return carry

    lax.fori_loop(1, nx, ask_x, 0)
    fin_ref[x_at] = comb_ref[x_at]
    finish(fin_ref, nx - 1, xr_sem)

    def send_group(first, at, source, target, send_sem, recv_sem):
        def send(step, carry):
            peer = at * nz + (z_at + near(step, nz)) % nz
            pltpu.make_async_remote_copy(
                src_ref=source.at[peer], dst_ref=target.at[emb], send_sem=send_sem, recv_sem=recv_sem,
                device_id={"emb": peer}, device_id_type=MESH,
            ).start()
            return carry

        lax.fori_loop(first, nz + first, send, 0) if first == 0 else lax.fori_loop(1, nz, send, 0)

    def blocks(value):
        left = value[:, :half].reshape(nz, CAP, half)
        right = value[:, half:].reshape(nz, CAP, half)
        return jnp.concatenate([left, right], axis=1).astype(BF16)

    def unblocks(value):
        value = value.astype(F32)
        left = value[:, :CAP].reshape(groups * CAP, half)
        right = value[:, CAP:].reshape(groups * CAP, half)
        return jnp.concatenate([left, right], axis=1).astype(BF16)

    loads[0].wait()

    def answer(step, first):
        at = (x_at + step) % nx
        asked = to_col(fin_ref[at])
        pick = (asked == (iota((lanes, rows), 1) + 1).astype(F32)).astype(BF16)
        for side in range(chunks):
            cols = slice(side * 2 * half, (side + 1) * 2 * half)
            send_ref[side, pl.ds(at * nz, nz)] = blocks(dot(pick, table_ref[:, cols]))
        for side in range(chunks):
            send_group(first, at, send_ref.at[side], recv_ref.at[side], rs_sem.at[side], rr_sem.at[side])

    answer(0, 1)

    def answer_other(step, carry):
        answer(step, 0)
        return carry

    lax.fori_loop(1, nx, answer_other, 0)
    for side in range(chunks):
        recv_ref[side, emb] = send_ref[side, emb]

    asked = jnp.concatenate([fin_ref[at] for at in range(nx)], axis=1)
    put_ref[...] = ((iota((rows, groups * CAP), 0) + 1).astype(F32) == asked).astype(BF16)

    for side in range(chunks):
        finish(recv_ref.at[side], groups - 1, rr_sem.at[side])
        cols = slice(side * 2 * half, (side + 1) * 2 * half)
        x_ref[:, cols] = dot(place_ref[...], unblocks(recv_ref[side])).astype(BF16)

    for load in loads[1:]:
        load.wait()
    forward_backward(seg_ref[...].astype(F32), x_ref, grad_ref, win_ref, wout_ref, mixed_ref, dx_ref,
                     proj_ref, slope_ref, weight_ref, wslope_ref, dz_ref)

    for side in range(chunks):
        cols = slice(side * 2 * half, (side + 1) * 2 * half)

        def give(step, first):
            at = (x_at + step) % nx
            mine = back_ref[pl.ds(pl.multiple_of(at * lanes, lanes), lanes), :]
            gsend_ref[side, pl.ds(at * nz, nz)] = blocks(dot(mine, dx_ref[:, cols]))
            send_group(first, at, gsend_ref.at[side], grecv_ref.at[side], gs_sem.at[side], gr_sem.at[side])

        give(0, 1)

        def give_other(step, carry):
            give(step, 0)
            return carry

        lax.fori_loop(1, nx, give_other, 0)
        grecv_ref[side, emb] = gsend_ref[side, emb]

    for side in range(chunks):
        finish(grecv_ref.at[side], groups - 1, gr_sem.at[side])
        dense = dot(put_ref[...], unblocks(grecv_ref[side]))
        dsend_ref[side] = dense.reshape(nd, rows // nd, 2 * half).astype(BF16)

        def send_dp(step, carry):
            peer = (dp + step) % nd
            pltpu.make_async_remote_copy(
                src_ref=dsend_ref.at[side, peer], dst_ref=drecv_ref.at[side, dp],
                send_sem=ds_sem.at[side], recv_sem=dr_sem.at[side],
                device_id={"dp": peer}, device_id_type=MESH,
            ).start()
            return carry

        lax.fori_loop(1, nd, send_dp, 0)
        drecv_ref[side, dp] = dsend_ref[side, dp]

    for side in range(chunks):
        finish(drecv_ref.at[side], nd - 1, dr_sem.at[side])
        cols = slice(side * 2 * half, (side + 1) * 2 * half)
        out_ref[:, cols] = jnp.sum(drecv_ref[side].astype(F32), axis=0)

    finish(ask_ref, nz - 1, zs_sem)
    finish(comb_ref, nx - 1, xs_sem)
    for side in range(chunks):
        finish(send_ref.at[side], groups - 1, rs_sem.at[side])
        finish(gsend_ref.at[side], groups - 1, gs_sem.at[side])
        finish(dsend_ref.at[side], nd - 1, ds_sem.at[side])


def layer(nx, nz, nd, table, item_shard, item_row, segment_ids, grad_out, w_in, w_out):
    tokens, width = grad_out.shape
    rows = table.shape[0]
    groups = nx * nz
    lanes = nz * CAP
    chunks = 1
    half = width // (2 * chunks)
    vmem = pl.BlockSpec(memory_space=pltpu.VMEM)
    anywhere = pl.BlockSpec(memory_space=pl.ANY)
    dma = pltpu.SemaphoreType.DMA
    pairs = HEADS // 2
    return pl.pallas_call(
        functools.partial(kernel, nx, nz, nd, chunks),
        out_shape=(
            jax.ShapeDtypeStruct((tokens, width), BF16),
            jax.ShapeDtypeStruct((rows // nd, width), F32),
        ),
        in_specs=[vmem] * 3 + [anywhere] * 4,
        out_specs=(vmem, vmem),
        scratch_shapes=[
            pltpu.VMEM((rows, width), BF16),
            pltpu.VMEM((tokens, width), BF16),
            pltpu.VMEM((width, 4 * width), BF16),
            pltpu.VMEM((width, width), BF16),
            pltpu.VMEM((nz, nx, lanes), F32),
            pltpu.VMEM((nz, nx, lanes), F32),
            pltpu.VMEM((nx, 1, lanes), F32),
            pltpu.VMEM((nx, 1, lanes), F32),
            pltpu.VMEM((tokens, groups * CAP), BF16),
            pltpu.VMEM((groups * CAP, tokens), BF16),
            pltpu.VMEM((rows, groups * CAP), BF16),
            pltpu.VMEM((chunks, groups, 2 * CAP, half), BF16),
            pltpu.VMEM((chunks, groups, 2 * CAP, half), BF16),
            pltpu.VMEM((tokens, width), BF16),
            pltpu.VMEM((tokens, width), BF16),
            pltpu.VMEM((tokens, 4 * width), BF16),
            pltpu.VMEM((tokens, 4 * width), F32),
            pltpu.VMEM((pairs, 2 * tokens, tokens), BF16),
            pltpu.VMEM((pairs, 2 * tokens, tokens), F32),
            pltpu.VMEM((tokens, 4 * width), BF16),
            pltpu.VMEM((chunks, groups, 2 * CAP, half), BF16),
            pltpu.VMEM((chunks, groups, 2 * CAP, half), BF16),
            pltpu.VMEM((chunks, nd, rows // nd, 2 * half), BF16),
            pltpu.VMEM((chunks, nd, rows // nd, 2 * half), BF16),
            dma((4,)), dma, dma, dma, dma,
            dma((chunks,)), dma((chunks,)), dma((chunks,)), dma((chunks,)), dma((chunks,)), dma((chunks,)),
        ],
        compiler_params=pltpu.CompilerParams(
            collective_id=0, has_side_effects=True, vmem_limit_bytes=48 * 2**20
        ),
        name="hstu",
    )(item_shard.reshape(1, tokens), item_row.reshape(1, tokens), segment_ids, table, grad_out, w_in, w_out)


def solution(mesh, nx=4):
    return jax.shard_map(
        functools.partial(layer, nx, mesh.shape["emb"] // nx, mesh.shape["dp"]),
        mesh=mesh,
        in_specs=(
            P("emb", None),
            P(("dp", "emb"), None),
            P(("dp", "emb")),
            P(("dp", "emb"), None),
            P(("dp", "emb"), None),
            P(),
            P(),
        ),
        out_specs=(P(("dp", "emb"), None), P(("emb", "dp"), None)),
        check_vma=False,
    )
```

```python
import functools

import jax
import jax.numpy as jnp
from jax import lax
from jax.experimental import pallas as pl
from jax.experimental.pallas import tpu as pltpu
from jax.sharding import PartitionSpec as P

HEADS = 8
CAP = 8
MOST = 128
MESH = pl.DeviceIdType.MESH
F32 = jnp.float32
BF16 = jnp.bfloat16


def dot(a, b, contract=(1, 0)):
    return lax.dot_general(
        a, b, (((contract[0],), (contract[1],)), ((), ())), preferred_element_type=F32
    )


def iota(shape, axis):
    return lax.broadcasted_iota(jnp.int32, shape, axis)


def to_col(row):
    n = row.shape[1]
    return jnp.sum(jnp.where(iota((n, n), 0) == iota((n, n), 1), row, 0.0), axis=1, keepdims=True)


def sigmoid(value):
    return 0.5 * jnp.tanh(0.5 * value) + 0.5


def near(step, size):
    return jnp.where(step % 2 == 1, (step + 1) // 2, size - step // 2)


def forward_backward(seg_row, x_ref, grad_ref, win_ref, wout_ref, gated_ref, dx_ref,
                     proj_ref, slope_ref, weight_ref, wslope_ref, dz_ref):
    tokens, width = x_ref.shape
    pairs = HEADS // 2
    lanes = 2 * width // HEADS
    scale = (width // HEADS) ** -0.5

    def part(index):
        return slice(index * width, (index + 1) * width)

    x = x_ref[...]
    for index in range(4):
        z = dot(x, win_ref[:, part(index)])
        sig = sigmoid(z)
        act = z * sig
        proj_ref[:, part(index)] = act.astype(BF16)
        slope_ref[:, part(index)] = sig + act * (1.0 - sig)

    seg_col = to_col(seg_row)
    seen = (iota((tokens, tokens), 1) <= iota((tokens, tokens), 0)) & (seg_col == seg_row)
    factor = jnp.where(seen, 1.0 / MOST, 0.0)
    factor = jnp.concatenate([factor, factor], axis=0)
    first = iota((tokens, lanes), 1) < lanes // 2

    def stack(value):
        zero = jnp.zeros_like(value)
        return jnp.concatenate([jnp.where(first, value, zero), jnp.where(first, zero, value)], axis=0)

    def unstack(value):
        return jnp.where(first, value[:tokens], value[tokens:])

    def pair(index, which):
        start = which * width + index * lanes
        return slice(start, start + lanes)

    attended = []
    for index in range(pairs):
        q = stack(proj_ref[:, pair(index, 2)])
        s = dot(q, proj_ref[:, pair(index, 3)], (1, 1)) * scale
        sig = sigmoid(s)
        act = s * sig
        weights = (act * factor).astype(BF16)
        weight_ref[index] = weights
        wslope_ref[index] = (sig + act * (1.0 - sig)) * (factor * scale)
        attended.append(unstack(dot(weights, proj_ref[:, pair(index, 1)])))
    attended = jnp.concatenate(attended, axis=1)

    center = attended - jnp.mean(attended, axis=1, keepdims=True)
    rstd = lax.rsqrt(jnp.mean(center * center, axis=1, keepdims=True) + 1e-05)
    normed = center * rstd
    u = proj_ref[:, part(0)].astype(F32)
    gated_ref[...] = (normed * u).astype(BF16)

    d_gated = dot(grad_ref[...], wout_ref[...], (1, 1)).astype(BF16).astype(F32)
    d_u = (d_gated * normed).astype(BF16).astype(F32)
    dz_ref[:, part(0)] = (d_u * slope_ref[:, part(0)]).astype(BF16)
    d_normed = d_gated * u
    d_att = rstd * (
        d_normed
        - jnp.mean(d_normed, axis=1, keepdims=True)
        - normed * jnp.mean(d_normed * normed, axis=1, keepdims=True)
    )
    d_att = d_att.astype(BF16)

    def put(index, which, value):
        value = value.astype(BF16).astype(F32)
        dz_ref[:, pair(index, which)] = (value * slope_ref[:, pair(index, which)]).astype(BF16)

    for index in range(pairs):
        q = stack(proj_ref[:, pair(index, 2)])
        d = stack(d_att[:, index * lanes:(index + 1) * lanes])
        put(index, 1, dot(weight_ref[index], d, (0, 0)))
        d_s = dot(d, proj_ref[:, pair(index, 1)], (1, 1)) * wslope_ref[index]
        d_s = d_s.astype(BF16)
        put(index, 2, unstack(dot(d_s, proj_ref[:, pair(index, 3)])))
        put(index, 3, dot(d_s, q, (0, 0)))

    d_x = dot(dz_ref[...], win_ref[...], (1, 1)).astype(BF16).astype(F32)
    dx_ref[...] = (d_x + grad_ref[...].astype(F32)).astype(BF16)


def kernel(nx, nz, nd, chunks,
           owner_hbm, row_hbm, seg_hbm, table_hbm, grad_hbm, win_hbm, wout_hbm,
           mixed_ref, out_ref,
           owner_ref, row_ref, seg_ref, table_ref, grad_ref, win_ref, wout_ref,
           ask_ref, mid_ref, comb_ref, fin_ref,
           place_ref, back_ref, put_ref,
           send_ref, recv_ref, x_ref, gated_ref, dx_ref,
           proj_ref, slope_ref, weight_ref, wslope_ref, dz_ref,
           gsend_ref, grecv_ref, dsend_ref, drecv_ref,
           load_sem, zs_sem, zr_sem, xs_sem, xr_sem, rs_sem, rr_sem, gs_sem, gr_sem, ds_sem, dr_sem):
    emb = lax.axis_index("emb")
    dp = lax.axis_index("dp")
    x_at, z_at = emb // nz, emb % nz
    groups = nx * nz
    tokens, width = x_ref.shape
    rows = table_ref.shape[0]
    lanes = nz * CAP

    loads = [
        pltpu.make_async_copy(source, target, load_sem.at[index])
        for index, (source, target) in enumerate(
            [(owner_hbm, owner_ref), (row_hbm, row_ref), (seg_hbm, seg_ref), (table_hbm, table_ref),
             (win_hbm, win_ref), (wout_hbm, wout_ref), (grad_hbm, grad_ref)]
        )
    ]
    for load in loads:
        load.start()

    barrier = pltpu.get_barrier_semaphore()

    def greet_z(step, carry):
        peer = x_at * nz + (z_at + step) % nz
        pl.semaphore_signal(barrier, 1, device_id={"emb": peer}, device_id_type=MESH)
        return carry

    def greet_x(step, carry):
        peer = (x_at + step) % nx * nz + z_at
        pl.semaphore_signal(barrier, 1, device_id={"emb": peer}, device_id_type=MESH)
        return carry

    def greet_dp(step, carry):
        pl.semaphore_signal(barrier, 1, device_id={"dp": (dp + step) % nd}, device_id_type=MESH)
        return carry

    lax.fori_loop(1, nz, greet_z, 0)
    lax.fori_loop(1, nx, greet_x, 0)
    lax.fori_loop(1, nd, greet_dp, 0)

    def finish(ref, count, sem):
        pltpu.make_async_copy(ref.at[pl.ds(0, count)], ref.at[pl.ds(0, count)], sem).wait()

    loads[0].wait()
    owner = owner_ref[...].astype(F32)
    named = iota((groups, tokens), 0).astype(F32) == owner
    before = (iota((tokens, tokens), 0) < iota((tokens, tokens), 1)).astype(BF16)
    named_bf = named.astype(BF16)
    slot = jnp.sum(jnp.where(named, dot(named_bf, before), 0.0), axis=0, keepdims=True)
    target = owner * CAP + slot
    place_ref[...] = (to_col(target) == iota((tokens, groups * CAP), 1).astype(F32)).astype(BF16)
    back_ref[...] = (iota((groups * CAP, tokens), 0).astype(F32) == target).astype(BF16)
    loads[1].wait()
    number = to_col((row_ref[...] + 1).astype(F32))
    lane = to_col(slot) + (z_at * CAP).astype(F32)
    here = lane == iota((tokens, lanes), 1).astype(F32)
    high = jnp.floor(number * (1.0 / 16.0))
    low = number - 16.0 * high
    ask = 16.0 * dot(named_bf, jnp.where(here, high, 0.0).astype(BF16)) + dot(
        named_bf, jnp.where(here, low, 0.0).astype(BF16)
    )
    for at in range(nx):
        ask_ref[:, pl.ds(at, 1), :] = ask[at * nz:(at + 1) * nz].reshape(nz, 1, lanes)

    pl.semaphore_wait(barrier, nz + nx + nd - 3)

    def ask_z(step, carry):
        peer = (z_at + near(step, nz)) % nz
        pltpu.make_async_remote_copy(
            src_ref=ask_ref.at[peer], dst_ref=mid_ref.at[z_at], send_sem=zs_sem, recv_sem=zr_sem,
            device_id={"emb": x_at * nz + peer}, device_id_type=MESH,
        ).start()
        return carry

    lax.fori_loop(1, nz, ask_z, 0)
    mid_ref[z_at] = ask_ref[z_at]
    finish(mid_ref, nz - 1, zr_sem)
    comb = jnp.sum(mid_ref[...], axis=0)
    for at in range(nx):
        comb_ref[at] = comb[at:at + 1]

    def ask_x(step, carry):
        peer = (x_at + step) % nx
        pltpu.make_async_remote_copy(
            src_ref=comb_ref.at[peer], dst_ref=fin_ref.at[x_at], send_sem=xs_sem, recv_sem=xr_sem,
            device_id={"emb": peer * nz + z_at}, device_id_type=MESH,
        ).start()
        return carry

    lax.fori_loop(1, nx, ask_x, 0)
    fin_ref[x_at] = comb_ref[x_at]
    finish(fin_ref, nx - 1, xr_sem)

    def send_group(first, at, source, target, send_sem, recv_sem):
        def send(step, carry):
            peer = at * nz + (z_at + near(step, nz)) % nz
            pltpu.make_async_remote_copy(
                src_ref=source.at[peer], dst_ref=target.at[emb], send_sem=send_sem, recv_sem=recv_sem,
                device_id={"emb": peer}, device_id_type=MESH,
            ).start()
            return carry

        lax.fori_loop(first, nz + first, send, 0) if first == 0 else lax.fori_loop(1, nz, send, 0)

    def blocks(value):
        half = value.shape[1] // 2
        left = value[:, :half].reshape(nz, CAP, half)
        right = value[:, half:].reshape(nz, CAP, half)
        return jnp.concatenate([left, right], axis=1).astype(BF16)

    def unblocks(value):
        half = value.shape[2]
        value = value.astype(F32)
        left = value[:, :CAP].reshape(groups * CAP, half)
        right = value[:, CAP:].reshape(groups * CAP, half)
        return jnp.concatenate([left, right], axis=1).astype(BF16)

    loads[3].wait()

    def answer(step, first):
        at = (x_at + step) % nx
        asked = to_col(fin_ref[at])
        pick = (asked == (iota((lanes, rows), 1) + 1).astype(F32)).astype(BF16)
        send_ref[pl.ds(at * nz, nz)] = blocks(dot(pick, table_ref[...]))
        send_group(first, at, send_ref, recv_ref, rs_sem, rr_sem)

    answer(0, 1)

    def answer_other(step, carry):
        answer(step, 0)
        return carry

    lax.fori_loop(1, nx, answer_other, 0)
    recv_ref[emb] = send_ref[emb]

    asked = jnp.concatenate([fin_ref[at] for at in range(nx)], axis=1)
    put_ref[...] = ((iota((rows, groups * CAP), 0) + 1).astype(F32) == asked).astype(BF16)

    finish(recv_ref, groups - 1, rr_sem)
    x_ref[...] = dot(place_ref[...], unblocks(recv_ref[...])).astype(BF16)

    for index in (2, 4, 5, 6):
        loads[index].wait()
    forward_backward(seg_ref[...].astype(F32), x_ref, grad_ref, win_ref, wout_ref, gated_ref, dx_ref,
                     proj_ref, slope_ref, weight_ref, wslope_ref, dz_ref)

    part = width // chunks
    for side in range(chunks):
        cols = slice(side * part, (side + 1) * part)

        def give(step, first):
            at = (x_at + step) % nx
            mine = back_ref[pl.ds(pl.multiple_of(at * lanes, lanes), lanes), :]
            gsend_ref[side, pl.ds(at * nz, nz)] = blocks(dot(mine, dx_ref[:, cols]))
            send_group(first, at, gsend_ref.at[side], grecv_ref.at[side], gs_sem.at[side], gr_sem.at[side])

        give(0, 1)

        def give_other(step, carry):
            give(step, 0)
            return carry

        lax.fori_loop(1, nx, give_other, 0)
        grecv_ref[side, emb] = gsend_ref[side, emb]

    mixed_ref[...] = (dot(gated_ref[...], wout_ref[...]) + x_ref[...].astype(F32)).astype(BF16)

    for side in range(chunks):
        finish(grecv_ref.at[side], groups - 1, gr_sem.at[side])
        dense = dot(put_ref[...], unblocks(grecv_ref[side]))
        dsend_ref[side] = dense.reshape(nd, rows // nd, part).astype(BF16)

        def send_dp(step, carry):
            peer = (dp + step) % nd
            pltpu.make_async_remote_copy(
                src_ref=dsend_ref.at[side, peer], dst_ref=drecv_ref.at[side, dp],
                send_sem=ds_sem.at[side], recv_sem=dr_sem.at[side],
                device_id={"dp": peer}, device_id_type=MESH,
            ).start()
            return carry

        lax.fori_loop(1, nd, send_dp, 0)
        drecv_ref[side, dp] = dsend_ref[side, dp]

    for side in range(chunks):
        finish(drecv_ref.at[side], nd - 1, dr_sem.at[side])
        cols = slice(side * part, (side + 1) * part)
        out_ref[:, cols] = jnp.sum(drecv_ref[side].astype(F32), axis=0)

    finish(ask_ref, nz - 1, zs_sem)
    finish(comb_ref, nx - 1, xs_sem)
    finish(send_ref, groups - 1, rs_sem)
    for side in range(chunks):
        finish(gsend_ref.at[side], groups - 1, gs_sem.at[side])
        finish(dsend_ref.at[side], nd - 1, ds_sem.at[side])


def layer(nx, nz, nd, table, item_shard, item_row, segment_ids, grad_out, w_in, w_out):
    tokens, width = grad_out.shape
    rows = table.shape[0]
    groups = nx * nz
    lanes = nz * CAP
    chunks = 2
    part = width // chunks
    vmem = pl.BlockSpec(memory_space=pltpu.VMEM)
    anywhere = pl.BlockSpec(memory_space=pl.ANY)
    dma = pltpu.SemaphoreType.DMA
    pairs = HEADS // 2
    return pl.pallas_call(
        functools.partial(kernel, nx, nz, nd, chunks),
        out_shape=(
            pltpu.VMEM((tokens, width), BF16),
            pltpu.VMEM((rows // nd, width), F32),
        ),
        in_specs=[anywhere] * 7,
        out_specs=(vmem, vmem),
        scratch_shapes=[
            pltpu.VMEM((1, tokens), jnp.int32),
            pltpu.VMEM((1, tokens), jnp.int32),
            pltpu.VMEM((1, tokens), jnp.int32),
            pltpu.VMEM((rows, width), BF16),
            pltpu.VMEM((tokens, width), BF16),
            pltpu.VMEM((width, 4 * width), BF16),
            pltpu.VMEM((width, width), BF16),
            pltpu.VMEM((nz, nx, lanes), F32),
            pltpu.VMEM((nz, nx, lanes), F32),
            pltpu.VMEM((nx, 1, lanes), F32),
            pltpu.VMEM((nx, 1, lanes), F32),
            pltpu.VMEM((tokens, groups * CAP), BF16),
            pltpu.VMEM((groups * CAP, tokens), BF16),
            pltpu.VMEM((rows, groups * CAP), BF16),
            pltpu.VMEM((groups, 2 * CAP, width // 2), BF16),
            pltpu.VMEM((groups, 2 * CAP, width // 2), BF16),
            pltpu.VMEM((tokens, width), BF16),
            pltpu.VMEM((tokens, width), BF16),
            pltpu.VMEM((tokens, width), BF16),
            pltpu.VMEM((tokens, 4 * width), BF16),
            pltpu.VMEM((tokens, 4 * width), F32),
            pltpu.VMEM((pairs, 2 * tokens, tokens), BF16),
            pltpu.VMEM((pairs, 2 * tokens, tokens), F32),
            pltpu.VMEM((tokens, 4 * width), BF16),
            pltpu.VMEM((chunks, groups, 2 * CAP, part // 2), BF16),
            pltpu.VMEM((chunks, groups, 2 * CAP, part // 2), BF16),
            pltpu.VMEM((chunks, nd, rows // nd, part), BF16),
            pltpu.VMEM((chunks, nd, rows // nd, part), BF16),
            dma((7,)), dma, dma, dma, dma,
            dma, dma, dma((chunks,)), dma((chunks,)), dma((chunks,)), dma((chunks,)),
        ],
        compiler_params=pltpu.CompilerParams(
            collective_id=0, has_side_effects=True, vmem_limit_bytes=60 * 2**20
        ),
        name="hstu",
    )(item_shard.reshape(1, tokens), item_row.reshape(1, tokens), segment_ids, table, grad_out, w_in, w_out)


def solution(mesh, nx=4):
    return jax.shard_map(
        functools.partial(layer, nx, mesh.shape["emb"] // nx, mesh.shape["dp"]),
        mesh=mesh,
        in_specs=(
            P("emb", None),
            P(("dp", "emb"), None),
            P(("dp", "emb")),
            P(("dp", "emb"), None),
            P(("dp", "emb"), None),
            P(),
            P(),
        ),
        out_specs=(P(("dp", "emb"), None), P(("emb", "dp"), None)),
        check_vma=False,
    )
```

```python
import functools

import jax
import jax.numpy as jnp
from jax import lax
from jax.experimental import pallas as pl
from jax.experimental.pallas import tpu as pltpu
from jax.sharding import PartitionSpec as P

HEADS = 8
CAP = 8
MOST = 128
MESH = pl.DeviceIdType.MESH
F32 = jnp.float32
BF16 = jnp.bfloat16


def dot(a, b, contract=(1, 0)):
    return lax.dot_general(
        a, b, (((contract[0],), (contract[1],)), ((), ())), preferred_element_type=F32
    )


def iota(shape, axis):
    return lax.broadcasted_iota(jnp.int32, shape, axis)


def to_col(row):
    n = row.shape[1]
    return jnp.sum(jnp.where(iota((n, n), 0) == iota((n, n), 1), row, 0.0), axis=1, keepdims=True)


def sigmoid(value):
    return 0.5 * jnp.tanh(0.5 * value) + 0.5


def ahead(at, distance, size):
    to = at + distance
    return jnp.where(to >= size, to - size, to)


def around(at, size, act):
    act(ahead(at, size // 2, size))

    def both(step, carry):
        distance = size // 2 - 1 - step
        act(ahead(at, distance, size))
        act(ahead(at, size - distance, size))
        return carry

    lax.fori_loop(0, size // 2 - 1, both, 0)


def forward_backward(seg_row, x_ref, grad_ref, win_ref, wout_ref, gated_ref, dx_ref,
                     proj_ref, slope_ref, weight_ref, wslope_ref, dz_ref):
    tokens, width = x_ref.shape
    pairs = HEADS // 2
    lanes = 2 * width // HEADS
    scale = (width // HEADS) ** -0.5

    def part(index):
        return slice(index * width, (index + 1) * width)

    x = x_ref[...]
    for index in range(4):
        z = dot(x, win_ref[:, part(index)])
        sig = sigmoid(z)
        act = z * sig
        proj_ref[:, part(index)] = act.astype(BF16)
        slope_ref[:, part(index)] = sig + act * (1.0 - sig)

    seg_col = to_col(seg_row)
    seen = (iota((tokens, tokens), 1) <= iota((tokens, tokens), 0)) & (seg_col == seg_row)
    factor = jnp.where(seen, 1.0 / MOST, 0.0)
    factor = jnp.concatenate([factor, factor], axis=0)
    first = iota((tokens, lanes), 1) < lanes // 2

    def stack(value):
        zero = jnp.zeros_like(value)
        return jnp.concatenate([jnp.where(first, value, zero), jnp.where(first, zero, value)], axis=0)

    def unstack(value):
        return jnp.where(first, value[:tokens], value[tokens:])

    def pair(index, which):
        start = which * width + index * lanes
        return slice(start, start + lanes)

    attended = []
    for index in range(pairs):
        q = stack(proj_ref[:, pair(index, 2)])
        s = dot(q, proj_ref[:, pair(index, 3)], (1, 1)) * scale
        sig = sigmoid(s)
        act = s * sig
        weights = (act * factor).astype(BF16)
        weight_ref[index] = weights
        wslope_ref[index] = (sig + act * (1.0 - sig)) * (factor * scale)
        attended.append(unstack(dot(weights, proj_ref[:, pair(index, 1)])))
    attended = jnp.concatenate(attended, axis=1)

    center = attended - jnp.mean(attended, axis=1, keepdims=True)
    rstd = lax.rsqrt(jnp.mean(center * center, axis=1, keepdims=True) + 1e-05)
    normed = center * rstd
    u = proj_ref[:, part(0)].astype(F32)
    gated_ref[...] = (normed * u).astype(BF16)

    d_gated = dot(grad_ref[...], wout_ref[...], (1, 1)).astype(BF16).astype(F32)
    d_u = (d_gated * normed).astype(BF16).astype(F32)
    dz_ref[:, part(0)] = (d_u * slope_ref[:, part(0)]).astype(BF16)
    d_normed = d_gated * u
    d_att = rstd * (
        d_normed
        - jnp.mean(d_normed, axis=1, keepdims=True)
        - normed * jnp.mean(d_normed * normed, axis=1, keepdims=True)
    )
    d_att = d_att.astype(BF16)

    def put(index, which, value):
        value = value.astype(BF16).astype(F32)
        dz_ref[:, pair(index, which)] = (value * slope_ref[:, pair(index, which)]).astype(BF16)

    for index in range(pairs):
        q = stack(proj_ref[:, pair(index, 2)])
        d = stack(d_att[:, index * lanes:(index + 1) * lanes])
        put(index, 1, dot(weight_ref[index], d, (0, 0)))
        d_s = dot(d, proj_ref[:, pair(index, 1)], (1, 1)) * wslope_ref[index]
        d_s = d_s.astype(BF16)
        put(index, 2, unstack(dot(d_s, proj_ref[:, pair(index, 3)])))
        put(index, 3, dot(d_s, q, (0, 0)))

    d_x = dot(dz_ref[...], win_ref[...], (1, 1)).astype(BF16).astype(F32)
    dx_ref[...] = (d_x + grad_ref[...].astype(F32)).astype(BF16)


def kernel(nx, nz, nd,
           owner_hbm, row_hbm, seg_hbm, table_hbm, grad_hbm, win_hbm, wout_hbm,
           mixed_ref, out_ref,
           owner_ref, row_ref, seg_ref, table_ref, grad_ref, win_ref, wout_ref,
           ask_ref, mid_ref, comb_ref, fin_ref, pask_ref, pmid_ref, pcomb_ref, pfin_ref,
           place_ref, back_ref, pback_ref, put_ref, pput_ref,
           send_ref, recv_ref, x_ref, gated_ref, dx_ref,
           proj_ref, slope_ref, weight_ref, wslope_ref, dz_ref,
           gsend_ref, grecv_ref, psend_ref, precv_ref, dsend_ref, drecv_ref, bsend_ref, brecv_ref,
           load_sem, zs_sem, zr_sem, xs_sem, xr_sem, ps_sem, pr_sem, qs_sem, qr_sem, rs_sem, rr_sem,
           gs_sem, gr_sem, hs_sem, hr_sem, ds_sem, dr_sem, bs_sem, br_sem):
    emb = lax.axis_index("emb")
    dp = lax.axis_index("dp")
    x_at, z_at = emb // nz, emb % nz
    groups = nx * nz
    tokens, width = x_ref.shape
    rows = table_ref.shape[0]
    lanes = nz * CAP

    barrier = pltpu.get_barrier_semaphore()

    def greet(peer, axis):
        pl.semaphore_signal(barrier, 1, device_id={axis: peer}, device_id_type=MESH)

    ny = nd // 2
    far = [way for step in range(ny // 2, 0, -1) for way in ((step, ny - step) if 2 * step < ny else (step,))]
    y_at, core_at = dp // 2, dp % 2
    k_at = y_at + ny * core_at
    plane = [(ahead(y_at, way, ny), core) for way in far for core in range(2)] + [(y_at, 1 - core_at)]
    plane = [(y * 2 + core, y + ny * core) for y, core in plane]
    dp_peers = [peer for peer, _ in plane]
    x_all = [ahead(x_at, step, nx) for step in range(nx)]

    around(z_at, nz, lambda to: greet(x_at * nz + to, "emb"))
    for to in x_all[1:]:
        greet(to * nz + z_at, "emb")
    for peer in dp_peers:
        greet(peer, "dp")

    loads = [
        pltpu.make_async_copy(source, target, load_sem.at[index])
        for index, (source, target) in enumerate(
            [(owner_hbm, owner_ref), (row_hbm, row_ref), (seg_hbm, seg_ref), (table_hbm, table_ref),
             (win_hbm, win_ref), (wout_hbm, wout_ref), (grad_hbm, grad_ref)]
        )
    ]
    for load in loads:
        load.start()

    def finish(ref, count, sem):
        pltpu.make_async_copy(ref.at[pl.ds(0, count)], ref.at[pl.ds(0, count)], sem).wait()

    loads[0].wait()
    owner = owner_ref[...].astype(F32)
    named = iota((groups, tokens), 0).astype(F32) == owner
    before = (iota((tokens, tokens), 0) < iota((tokens, tokens), 1)).astype(BF16)
    named_bf = named.astype(BF16)
    slot = jnp.sum(jnp.where(named, dot(named_bf, before), 0.0), axis=0, keepdims=True)
    target = owner * CAP + slot
    loads[1].wait()
    number = to_col((row_ref[...] + 1).astype(F32))
    slot_col = to_col(slot)
    lane_at = iota((tokens, lanes), 1).astype(F32)
    here = slot_col + (z_at * CAP).astype(F32) == lane_at
    high = jnp.floor(number * (1.0 / 16.0))
    low = number - 16.0 * high

    def numbers(named_bf, here):
        return 16.0 * dot(named_bf, jnp.where(here, high, 0.0).astype(BF16)) + dot(
            named_bf, jnp.where(here, low, 0.0).astype(BF16)
        )

    ask = numbers(named_bf, here)
    for at in range(nx):
        ask_ref[:, pl.ds(at, 1), :] = ask[at * nz:(at + 1) * nz].reshape(nz, 1, lanes)

    pl.semaphore_wait(barrier, nz + nx + nd - 3)

    def ask_z(peer):
        pltpu.make_async_remote_copy(
            src_ref=ask_ref.at[peer], dst_ref=mid_ref.at[z_at], send_sem=zs_sem, recv_sem=zr_sem,
            device_id={"emb": x_at * nz + peer}, device_id_type=MESH,
        ).start()

    around(z_at, nz, ask_z)
    mid_ref[z_at] = ask_ref[z_at]

    owner_x = jnp.floor(owner * (1.0 / nz))
    ahead_z = owner - nz * owner_x - z_at.astype(F32)
    ahead_z = jnp.where(ahead_z < 0.0, ahead_z + nz, ahead_z)
    behind_z = jnp.where(ahead_z > 0.0, nz - ahead_z, 0.0)
    served = [owner_x * nz + ahead_z, owner_x * nz + behind_z]
    here = slot_col + (dp * CAP).astype(F32) == lane_at
    device = iota((groups, tokens), 0).astype(F32)
    pask = numbers(jnp.concatenate([device == one for one in served], axis=0).astype(BF16), here)
    for at in range(2 * nx):
        pask_ref[:, pl.ds(at, 1), :] = pask[at % 2 * groups + at // 2 * nz:][:nz].reshape(nz, 1, lanes)
    for peer, k in plane:
        pltpu.make_async_remote_copy(
            src_ref=pask_ref.at[k], dst_ref=pmid_ref.at[dp], send_sem=ps_sem, recv_sem=pr_sem,
            device_id={"dp": peer}, device_id_type=MESH,
        ).start()
    pmid_ref[dp] = pask_ref[k_at]

    finish(mid_ref, nz - 1, zr_sem)
    comb = jnp.sum(mid_ref[...], axis=0)
    for at in range(nx):
        comb_ref[at] = comb[at:at + 1]

    for peer in x_all[1:]:
        pltpu.make_async_remote_copy(
            src_ref=comb_ref.at[peer], dst_ref=fin_ref.at[x_at], send_sem=xs_sem, recv_sem=xr_sem,
            device_id={"emb": peer * nz + z_at}, device_id_type=MESH,
        ).start()
    fin_ref[x_at] = comb_ref[x_at]

    finish(pmid_ref, nd - 1, pr_sem)
    pcomb = jnp.sum(pmid_ref[...], axis=0)
    for at in range(nx):
        pcomb_ref[at] = pcomb[2 * at:2 * at + 2]
    for peer in x_all[1:]:
        pltpu.make_async_remote_copy(
            src_ref=pcomb_ref.at[peer], dst_ref=pfin_ref.at[x_at], send_sem=qs_sem, recv_sem=qr_sem,
            device_id={"emb": peer * nz + z_at}, device_id_type=MESH,
        ).start()
    pfin_ref[x_at] = pcomb_ref[x_at]

    def send_all(places, source, target, send_sem, recv_sem):
        def send(peer):
            pltpu.make_async_remote_copy(
                src_ref=source.at[peer], dst_ref=target.at[emb], send_sem=send_sem, recv_sem=recv_sem,
                device_id={"emb": peer}, device_id_type=MESH,
            ).start()

        def send_z(to):
            for at in places:
                send(at * nz + to)

        around(z_at, nz, send_z)
        for at in places:
            if at is not x_all[0]:
                send(at * nz + z_at)

    def blocks(value):
        half = value.shape[1] // 2
        left = value[:, :half].reshape(nz, CAP, half)
        right = value[:, half:].reshape(nz, CAP, half)
        return jnp.concatenate([left, right], axis=1).astype(BF16)

    def together(value):
        return jnp.concatenate([blocks(value[at * lanes:(at + 1) * lanes]) for at in range(nx)], axis=0)

    def unblocks(value):
        half = value.shape[2]
        value = value.astype(F32)
        left = value[:, :CAP].reshape(groups * CAP, half)
        right = value[:, CAP:].reshape(groups * CAP, half)
        return jnp.concatenate([left, right], axis=1).astype(BF16)

    loads[3].wait()

    def answer(at):
        asked = to_col(fin_ref[at])
        pick = (asked == (iota((lanes, rows), 1) + 1).astype(F32)).astype(BF16)
        send_ref[pl.ds(at * nz, nz)] = blocks(dot(pick, table_ref[...]))

    answer(x_at)
    send_all(x_all[:1], send_ref, recv_ref, rs_sem, rr_sem)
    finish(fin_ref, nx - 1, xr_sem)
    for at in x_all[1:]:
        answer(at)
    send_all(x_all[1:], send_ref, recv_ref, rs_sem, rr_sem)
    recv_ref[emb] = send_ref[emb]

    place_ref[...] = (to_col(target) == iota((tokens, groups * CAP), 1).astype(F32)).astype(BF16)
    at_slot = iota((groups * CAP, tokens), 0).astype(F32)
    back_ref[...] = (at_slot == target).astype(BF16)
    for which in range(2):
        pback_ref[which] = (at_slot == served[which] * CAP + slot).astype(BF16)
    at_row = (iota((rows, groups * CAP), 0) + 1).astype(F32)
    put_ref[...] = (at_row == jnp.concatenate([fin_ref[at] for at in range(nx)], axis=1)).astype(BF16)
    finish(pfin_ref, nx - 1, qr_sem)
    for which in range(2):
        asked = jnp.concatenate([pfin_ref[at][which:which + 1] for at in range(nx)], axis=1)
        pput_ref[which] = (at_row == asked).astype(BF16)

    finish(recv_ref, groups - 1, rr_sem)
    x_ref[...] = dot(place_ref[...], unblocks(recv_ref[...])).astype(BF16)

    for index in (2, 4, 5, 6):
        loads[index].wait()
    forward_backward(seg_ref[...].astype(F32), x_ref, grad_ref, win_ref, wout_ref, gated_ref, dx_ref,
                     proj_ref, slope_ref, weight_ref, wslope_ref, dz_ref)

    part = width // 2
    quarter = part // 2
    gsend_ref[...] = together(dot(back_ref[...], dx_ref[:, :part]))
    send_all(x_all, gsend_ref, grecv_ref, gs_sem, gr_sem)
    grecv_ref[emb] = gsend_ref[emb]

    given = [dot(pback_ref[which], dx_ref[:, part + which * quarter:][:, :quarter]) for which in range(2)]
    psend_ref[...] = together(jnp.concatenate(given, axis=1))
    for peer, k in plane + [(dp, k_at)]:
        for at in x_all:
            if peer is dp and at is x_all[0]:
                continue
            pltpu.make_async_remote_copy(
                src_ref=psend_ref.at[at * nz + k], dst_ref=precv_ref.at[x_at * nd + dp],
                send_sem=hs_sem, recv_sem=hr_sem,
                device_id={"dp": peer, "emb": at * nz + z_at}, device_id_type=MESH,
            ).start()
    precv_ref[x_at * nd + dp] = psend_ref[x_at * nz + k_at]

    mixed_ref[...] = (dot(gated_ref[...], wout_ref[...]) + x_ref[...].astype(F32)).astype(BF16)

    finish(precv_ref, groups - 1, hr_sem)
    taken = unblocks(precv_ref[...])
    for which in range(2):
        dense = dot(pput_ref[which], taken[:, which * quarter:(which + 1) * quarter])
        bsend_ref[which] = dense.reshape(nd, rows // nd, quarter).astype(BF16)
    homes = [x_at * nz + ahead(z_at, k_at, nz), x_at * nz + ahead(z_at, jnp.where(k_at > 0, nz - k_at, 0), nz)]

    def home(which, peer):
        return pltpu.make_async_remote_copy(
            src_ref=bsend_ref.at[which, peer], dst_ref=brecv_ref.at[which, z_at],
            send_sem=bs_sem.at[which], recv_sem=br_sem.at[which],
            device_id={"dp": peer, "emb": homes[which]}, device_id_type=MESH,
        )

    for peer in dp_peers:
        for which in range(2):
            home(which, peer).start()

    @pl.when(k_at > 0)
    def _():
        for which in range(2):
            home(which, dp).start()

    @pl.when(k_at == 0)
    def _():
        for which in range(2):
            pltpu.make_async_copy(
                bsend_ref.at[which, dp], brecv_ref.at[which, z_at], br_sem.at[which]
            ).start()

    finish(grecv_ref, groups - 1, gr_sem)
    dense = dot(put_ref[...], unblocks(grecv_ref[...]))
    dsend_ref[...] = dense.reshape(nd, rows // nd, part).astype(BF16)
    for peer in dp_peers:
        pltpu.make_async_remote_copy(
            src_ref=dsend_ref.at[peer], dst_ref=drecv_ref.at[dp], send_sem=ds_sem, recv_sem=dr_sem,
            device_id={"dp": peer}, device_id_type=MESH,
        ).start()
    drecv_ref[dp] = dsend_ref[dp]

    finish(drecv_ref, nd - 1, dr_sem)
    out_ref[:, :part] = jnp.sum(drecv_ref[...].astype(F32), axis=0)
    for which in range(2):
        finish(brecv_ref.at[which], nz, br_sem.at[which])
        cols = slice(part + which * quarter, part + (which + 1) * quarter)
        out_ref[:, cols] = jnp.sum(brecv_ref[which].astype(F32), axis=0)

    finish(ask_ref, nz - 1, zs_sem)
    finish(comb_ref, nx - 1, xs_sem)
    finish(pask_ref, nd - 1, ps_sem)
    finish(pcomb_ref, nx - 1, qs_sem)
    finish(send_ref, groups - 1, rs_sem)
    finish(gsend_ref, groups - 1, gs_sem)
    finish(psend_ref, groups - 1, hs_sem)
    finish(dsend_ref, nd - 1, ds_sem)
    for which in range(2):
        finish(bsend_ref.at[which], nd - 1, bs_sem.at[which])

    @pl.when(k_at > 0)
    def _():
        for which in range(2):
            finish(bsend_ref.at[which], 1, bs_sem.at[which])


def layer(nx, nz, nd, table, item_shard, item_row, segment_ids, grad_out, w_in, w_out):
    tokens, width = grad_out.shape
    rows = table.shape[0]
    groups = nx * nz
    lanes = nz * CAP
    part = width // 2
    quarter = part // 2
    vmem = pl.BlockSpec(memory_space=pltpu.VMEM)
    anywhere = pl.BlockSpec(memory_space=pl.ANY)
    dma = pltpu.SemaphoreType.DMA
    pairs = HEADS // 2
    return pl.pallas_call(
        functools.partial(kernel, nx, nz, nd),
        out_shape=(
            pltpu.VMEM((tokens, width), BF16),
            pltpu.VMEM((rows // nd, width), F32),
        ),
        in_specs=[anywhere] * 7,
        out_specs=(vmem, vmem),
        scratch_shapes=[
            pltpu.VMEM((1, tokens), jnp.int32),
            pltpu.VMEM((1, tokens), jnp.int32),
            pltpu.VMEM((1, tokens), jnp.int32),
            pltpu.VMEM((rows, width), BF16),
            pltpu.VMEM((tokens, width), BF16),
            pltpu.VMEM((width, 4 * width), BF16),
            pltpu.VMEM((width, width), BF16),
            pltpu.VMEM((nz, nx, lanes), F32),
            pltpu.VMEM((nz, nx, lanes), F32),
            pltpu.VMEM((nx, 1, lanes), F32),
            pltpu.VMEM((nx, 1, lanes), F32),
            pltpu.VMEM((nz, 2 * nx, lanes), F32),
            pltpu.VMEM((nd, 2 * nx, lanes), F32),
            pltpu.VMEM((nx, 2, lanes), F32),
            pltpu.VMEM((nx, 2, lanes), F32),
            pltpu.VMEM((tokens, groups * CAP), BF16),
            pltpu.VMEM((groups * CAP, tokens), BF16),
            pltpu.VMEM((2, groups * CAP, tokens), BF16),
            pltpu.VMEM((rows, groups * CAP), BF16),
            pltpu.VMEM((2, rows, groups * CAP), BF16),
            pltpu.VMEM((groups, 2 * CAP, width // 2), BF16),
            pltpu.VMEM((groups, 2 * CAP, width // 2), BF16),
            pltpu.VMEM((tokens, width), BF16),
            pltpu.VMEM((tokens, width), BF16),
            pltpu.VMEM((tokens, width), BF16),
            pltpu.VMEM((tokens, 4 * width), BF16),
            pltpu.VMEM((tokens, 4 * width), F32),
            pltpu.VMEM((pairs, 2 * tokens, tokens), BF16),
            pltpu.VMEM((pairs, 2 * tokens, tokens), F32),
            pltpu.VMEM((tokens, 4 * width), BF16),
            pltpu.VMEM((groups, 2 * CAP, quarter), BF16),
            pltpu.VMEM((groups, 2 * CAP, quarter), BF16),
            pltpu.VMEM((groups, 2 * CAP, quarter), BF16),
            pltpu.VMEM((groups, 2 * CAP, quarter), BF16),
            pltpu.VMEM((nd, rows // nd, part), BF16),
            pltpu.VMEM((nd, rows // nd, part), BF16),
            pltpu.VMEM((2, nd, rows // nd, quarter), BF16),
            pltpu.VMEM((2, nz, rows // nd, quarter), BF16),
            dma((7,)),
        ]
        + [dma] * 16
        + [dma((2,))] * 2,
        compiler_params=pltpu.CompilerParams(
            collective_id=0, has_side_effects=True, vmem_limit_bytes=60 * 2**20
        ),
        name="hstu",
    )(item_shard.reshape(1, tokens), item_row.reshape(1, tokens), segment_ids, table, grad_out, w_in, w_out)


def solution(mesh, nx=4):
    return jax.shard_map(
        functools.partial(layer, nx, mesh.shape["emb"] // nx, mesh.shape["dp"]),
        mesh=mesh,
        in_specs=(
            P("emb", None),
            P(("dp", "emb"), None),
            P(("dp", "emb")),
            P(("dp", "emb"), None),
            P(("dp", "emb"), None),
            P(),
            P(),
        ),
        out_specs=(P(("dp", "emb"), None), P(("emb", "dp"), None)),
        check_vma=False,
    )
```

```python
import functools

import jax
import jax.numpy as jnp
from jax import lax
from jax.experimental import pallas as pl
from jax.experimental.pallas import tpu as pltpu
from jax.sharding import PartitionSpec as P

HEADS = 8
CAP = 8
MOST = 128
MESH = pl.DeviceIdType.MESH
F32 = jnp.float32
BF16 = jnp.bfloat16


def dot(a, b, contract=(1, 0)):
    return lax.dot_general(
        a, b, (((contract[0],), (contract[1],)), ((), ())), preferred_element_type=F32
    )


def iota(shape, axis):
    return lax.broadcasted_iota(jnp.int32, shape, axis)


def to_col(row):
    n = row.shape[1]
    return jnp.sum(jnp.where(iota((n, n), 0) == iota((n, n), 1), row, 0.0), axis=1, keepdims=True)


def sigmoid(value):
    return 0.5 * jnp.tanh(0.5 * value) + 0.5


def ahead(at, distance, size):
    to = at + distance
    return jnp.where(to >= size, to - size, to)


def around(at, size, act):
    act(ahead(at, size // 2, size))

    def both(step, carry):
        distance = size // 2 - 1 - step
        act(ahead(at, distance, size))
        act(ahead(at, size - distance, size))
        return carry

    lax.fori_loop(0, size // 2 - 1, both, 0)


def forward_backward(factor_ref, d_gated_ref, x_ref, win_ref, gated_ref,
                     proj_ref, slope_ref, weight_ref, wslope_ref, dz_ref):
    tokens, width = x_ref.shape
    pairs = HEADS // 2
    lanes = 2 * width // HEADS
    scale = (width // HEADS) ** -0.5

    def part(index):
        return slice(index * width, (index + 1) * width)

    x = x_ref[...]
    for index in range(4):
        z = dot(x, win_ref[:, part(index)])
        sig = sigmoid(z)
        act = z * sig
        proj_ref[:, part(index)] = act.astype(BF16)
        slope_ref[:, part(index)] = sig + act * (1.0 - sig)

    factor = factor_ref[...]
    factor = jnp.concatenate([factor, factor], axis=0)
    first = iota((tokens, lanes), 1) < lanes // 2

    def stack(value):
        zero = jnp.zeros_like(value)
        return jnp.concatenate([jnp.where(first, value, zero), jnp.where(first, zero, value)], axis=0)

    def unstack(value):
        return jnp.where(first, value[:tokens], value[tokens:])

    def pair(index, which):
        start = which * width + index * lanes
        return slice(start, start + lanes)

    attended = []
    for index in range(pairs):
        q = stack(proj_ref[:, pair(index, 2)])
        s = dot(q, proj_ref[:, pair(index, 3)], (1, 1)) * scale
        sig = sigmoid(s)
        act = s * sig
        weights = (act * factor).astype(BF16)
        weight_ref[index] = weights
        wslope_ref[index] = (sig + act * (1.0 - sig)) * (factor * scale)
        attended.append(unstack(dot(weights, proj_ref[:, pair(index, 1)])))
    attended = jnp.concatenate(attended, axis=1)

    center = attended - jnp.mean(attended, axis=1, keepdims=True)
    rstd = lax.rsqrt(jnp.mean(center * center, axis=1, keepdims=True) + 1e-05)
    normed = center * rstd
    u = proj_ref[:, part(0)].astype(F32)
    gated_ref[...] = (normed * u).astype(BF16)

    d_gated = d_gated_ref[...].astype(F32)
    d_u = (d_gated * normed).astype(BF16).astype(F32)
    dz_ref[:, part(0)] = (d_u * slope_ref[:, part(0)]).astype(BF16)
    d_normed = d_gated * u
    d_att = rstd * (
        d_normed
        - jnp.mean(d_normed, axis=1, keepdims=True)
        - normed * jnp.mean(d_normed * normed, axis=1, keepdims=True)
    )
    d_att = d_att.astype(BF16)

    def put(index, which, value):
        value = value.astype(BF16).astype(F32)
        dz_ref[:, pair(index, which)] = (value * slope_ref[:, pair(index, which)]).astype(BF16)

    for index in range(pairs):
        q = stack(proj_ref[:, pair(index, 2)])
        d = stack(d_att[:, index * lanes:(index + 1) * lanes])
        put(index, 1, dot(weight_ref[index], d, (0, 0)))
        d_s = dot(d, proj_ref[:, pair(index, 1)], (1, 1)) * wslope_ref[index]
        d_s = d_s.astype(BF16)
        put(index, 2, unstack(dot(d_s, proj_ref[:, pair(index, 3)])))
        put(index, 3, dot(d_s, q, (0, 0)))


def kernel(nx, nz, nd,
           owner_hbm, row_hbm, seg_hbm, table_hbm, grad_hbm, win_hbm, wout_hbm,
           mixed_ref, out_ref,
           owner_ref, row_ref, seg_ref, table_ref, grad_ref, win_ref, wout_ref,
           ask_ref, mid_ref, comb_ref, fin_ref, pask_ref, pmid_ref, pcomb_ref, pfin_ref,
           place_ref, back_ref, pback_ref, put_ref, pput_ref,
           send_ref, recv_ref, x_ref, gated_ref, factor_ref, d_gated_ref, wint_ref,
           proj_ref, slope_ref, weight_ref, wslope_ref, dz_ref,
           gsend_ref, grecv_ref, psend_ref, precv_ref, dsend_ref, drecv_ref, bsend_ref, brecv_ref,
           load_sem, zs_sem, zr_sem, xs_sem, xr_sem, ps_sem, pr_sem, qs_sem, qr_sem, rs_sem, rr_sem,
           gs_sem, gr_sem, hs_sem, hr_sem, ds_sem, dr_sem, bs_sem, br_sem):
    emb = lax.axis_index("emb")
    dp = lax.axis_index("dp")
    x_at, z_at = emb // nz, emb % nz
    groups = nx * nz
    tokens, width = x_ref.shape
    rows = table_ref.shape[0]
    lanes = nz * CAP

    loads = [
        pltpu.make_async_copy(source, target, load_sem.at[index])
        for index, (source, target) in enumerate(
            [(owner_hbm, owner_ref), (row_hbm, row_ref), (seg_hbm, seg_ref), (table_hbm, table_ref),
             (win_hbm, win_ref), (wout_hbm, wout_ref), (grad_hbm, grad_ref)]
        )
    ]
    for load in loads[:2]:
        load.start()

    barrier = pltpu.get_barrier_semaphore()

    def greet(peer, axis):
        pl.semaphore_signal(barrier, 1, device_id={axis: peer}, device_id_type=MESH)

    ny = nd // 2
    far = [way for step in range(ny // 2, 0, -1) for way in ((step, ny - step) if 2 * step < ny else (step,))]
    y_at, core_at = dp // 2, dp % 2
    k_at = y_at + ny * core_at
    plane = [(ahead(y_at, way, ny), core) for way in far for core in range(2)] + [(y_at, 1 - core_at)]
    plane = [(y * 2 + core, y + ny * core) for y, core in plane]
    dp_peers = [peer for peer, _ in plane]
    x_all = [ahead(x_at, step, nx) for step in range(nx)]

    around(z_at, nz, lambda to: greet(x_at * nz + to, "emb"))
    for to in x_all[1:]:
        greet(to * nz + z_at, "emb")
    for peer in dp_peers:
        greet(peer, "dp")
    for load in loads[2:]:
        load.start()

    def finish(ref, count, sem):
        pltpu.make_async_copy(ref.at[pl.ds(0, count)], ref.at[pl.ds(0, count)], sem).wait()

    loads[0].wait()
    owner = owner_ref[...].astype(F32)
    named = iota((groups, tokens), 0).astype(F32) == owner
    before = (iota((tokens, tokens), 0) < iota((tokens, tokens), 1)).astype(BF16)
    named_bf = named.astype(BF16)
    slot = jnp.sum(jnp.where(named, dot(named_bf, before), 0.0), axis=0, keepdims=True)
    target = owner * CAP + slot
    loads[1].wait()
    number = to_col((row_ref[...] + 1).astype(F32))
    slot_col = to_col(slot)
    lane_at = iota((tokens, lanes), 1).astype(F32)
    here = slot_col + (z_at * CAP).astype(F32) == lane_at
    high = jnp.floor(number * (1.0 / 16.0))
    low = number - 16.0 * high

    def numbers(named_bf, here):
        return 16.0 * dot(named_bf, jnp.where(here, high, 0.0).astype(BF16)) + dot(
            named_bf, jnp.where(here, low, 0.0).astype(BF16)
        )

    ask = numbers(named_bf, here)
    for at in range(nx):
        ask_ref[:, pl.ds(at, 1), :] = ask[at * nz:(at + 1) * nz].reshape(nz, 1, lanes)

    pl.semaphore_wait(barrier, nz + nx + nd - 3)

    def ask_z(peer):
        pltpu.make_async_remote_copy(
            src_ref=ask_ref.at[peer], dst_ref=mid_ref.at[z_at], send_sem=zs_sem, recv_sem=zr_sem,
            device_id={"emb": x_at * nz + peer}, device_id_type=MESH,
        ).start()

    around(z_at, nz, ask_z)
    mid_ref[z_at] = ask_ref[z_at]

    finish(mid_ref, nz - 1, zr_sem)
    comb = jnp.sum(mid_ref[...], axis=0)
    for at in range(nx):
        comb_ref[at] = comb[at:at + 1]

    for peer in x_all[1:]:
        pltpu.make_async_remote_copy(
            src_ref=comb_ref.at[peer], dst_ref=fin_ref.at[x_at], send_sem=xs_sem, recv_sem=xr_sem,
            device_id={"emb": peer * nz + z_at}, device_id_type=MESH,
        ).start()
    fin_ref[x_at] = comb_ref[x_at]

    def send_all(places, source, target, send_sem, recv_sem):
        def send(peer):
            pltpu.make_async_remote_copy(
                src_ref=source.at[peer], dst_ref=target.at[emb], send_sem=send_sem, recv_sem=recv_sem,
                device_id={"emb": peer}, device_id_type=MESH,
            ).start()

        def send_z(to):
            for at in places:
                send(at * nz + to)

        around(z_at, nz, send_z)
        for at in places:
            if at is not x_all[0]:
                send(at * nz + z_at)

    def blocks(value):
        half = value.shape[1] // 2
        left = value[:, :half].reshape(nz, CAP, half)
        right = value[:, half:].reshape(nz, CAP, half)
        return jnp.concatenate([left, right], axis=1).astype(BF16)

    def together(value):
        return jnp.concatenate([blocks(value[at * lanes:(at + 1) * lanes]) for at in range(nx)], axis=0)

    def unblocks(value):
        half = value.shape[2]
        value = value.astype(F32)
        left = value[:, :CAP].reshape(groups * CAP, half)
        right = value[:, CAP:].reshape(groups * CAP, half)
        return jnp.concatenate([left, right], axis=1).astype(BF16)

    loads[3].wait()

    def answer(at):
        asked = to_col(fin_ref[at])
        pick = (asked == (iota((lanes, rows), 1) + 1).astype(F32)).astype(BF16)
        send_ref[pl.ds(at * nz, nz)] = blocks(dot(pick, table_ref[...]))

    answer(x_at)
    send_all(x_all[:1], send_ref, recv_ref, rs_sem, rr_sem)
    finish(fin_ref, nx - 1, xr_sem)
    for at in x_all[1:]:
        answer(at)
    send_all(x_all[1:], send_ref, recv_ref, rs_sem, rr_sem)
    recv_ref[emb] = send_ref[emb]

    owner_x = jnp.floor(owner * (1.0 / nz))
    ahead_z = owner - nz * owner_x - z_at.astype(F32)
    ahead_z = jnp.where(ahead_z < 0.0, ahead_z + nz, ahead_z)
    behind_z = jnp.where(ahead_z > 0.0, nz - ahead_z, 0.0)
    served = [owner_x * nz + ahead_z, owner_x * nz + behind_z]
    here = slot_col + (dp * CAP).astype(F32) == lane_at
    device = iota((groups, tokens), 0).astype(F32)
    pask = numbers(jnp.concatenate([device == one for one in served], axis=0).astype(BF16), here)
    for at in range(2 * nx):
        pask_ref[:, pl.ds(at, 1), :] = pask[at % 2 * groups + at // 2 * nz:][:nz].reshape(nz, 1, lanes)
    for peer, k in plane:
        pltpu.make_async_remote_copy(
            src_ref=pask_ref.at[k], dst_ref=pmid_ref.at[dp], send_sem=ps_sem, recv_sem=pr_sem,
            device_id={"dp": peer}, device_id_type=MESH,
        ).start()
    pmid_ref[dp] = pask_ref[k_at]

    place_ref[...] = (to_col(target) == iota((tokens, groups * CAP), 1).astype(F32)).astype(BF16)
    at_slot = iota((groups * CAP, tokens), 0).astype(F32)
    back_ref[...] = (at_slot == target).astype(BF16)
    for which in range(2):
        pback_ref[which] = (at_slot == served[which] * CAP + slot).astype(BF16)
    at_row = (iota((rows, groups * CAP), 0) + 1).astype(F32)
    put_ref[...] = (at_row == jnp.concatenate([fin_ref[at] for at in range(nx)], axis=1)).astype(BF16)
    for index in (2, 4, 5, 6):
        loads[index].wait()
    seg_row = seg_ref[...].astype(F32)
    seen = (iota((tokens, tokens), 1) <= iota((tokens, tokens), 0)) & (to_col(seg_row) == seg_row)
    factor_ref[...] = jnp.where(seen, 1.0 / MOST, 0.0)
    wint_ref[...] = win_ref[...].T
    d_gated_ref[...] = dot(grad_ref[...], wout_ref[...], (1, 1)).astype(BF16)

    finish(recv_ref, groups - 1, rr_sem)
    x_ref[...] = dot(place_ref[...], unblocks(recv_ref[...])).astype(BF16)

    forward_backward(factor_ref, d_gated_ref, x_ref, win_ref, gated_ref,
                     proj_ref, slope_ref, weight_ref, wslope_ref, dz_ref)

    finish(pmid_ref, nd - 1, pr_sem)
    pcomb = jnp.sum(pmid_ref[...], axis=0)
    for at in range(nx):
        pcomb_ref[at] = pcomb[2 * at:2 * at + 2]
    for peer in x_all[1:]:
        pltpu.make_async_remote_copy(
            src_ref=pcomb_ref.at[peer], dst_ref=pfin_ref.at[x_at], send_sem=qs_sem, recv_sem=qr_sem,
            device_id={"emb": peer * nz + z_at}, device_id_type=MESH,
        ).start()
    pfin_ref[x_at] = pcomb_ref[x_at]

    part = width // 2
    quarter = part // 2

    def d_x(cols):
        value = dot(dz_ref[...], wint_ref[:, cols]).astype(BF16).astype(F32)
        return (value + grad_ref[:, cols].astype(F32)).astype(BF16)

    gsend_ref[...] = together(dot(back_ref[...], d_x(slice(0, part))))
    send_all(x_all, gsend_ref, grecv_ref, gs_sem, gr_sem)
    grecv_ref[emb] = gsend_ref[emb]

    right = d_x(slice(part, width))
    given = [dot(pback_ref[which], right[:, which * quarter:(which + 1) * quarter]) for which in range(2)]
    psend_ref[...] = together(jnp.concatenate(given, axis=1))
    for peer, k in plane + [(dp, k_at)]:
        for at in x_all:
            if peer is dp and at is x_all[0]:
                continue
            pltpu.make_async_remote_copy(
                src_ref=psend_ref.at[at * nz + k], dst_ref=precv_ref.at[x_at * nd + dp],
                send_sem=hs_sem, recv_sem=hr_sem,
                device_id={"dp": peer, "emb": at * nz + z_at}, device_id_type=MESH,
            ).start()
    precv_ref[x_at * nd + dp] = psend_ref[x_at * nz + k_at]

    mixed_ref[...] = (dot(gated_ref[...], wout_ref[...]) + x_ref[...].astype(F32)).astype(BF16)

    finish(pfin_ref, nx - 1, qr_sem)
    at_row = (iota((rows, groups * CAP), 0) + 1).astype(F32)
    for which in range(2):
        asked = jnp.concatenate([pfin_ref[at][which:which + 1] for at in range(nx)], axis=1)
        pput_ref[which] = (at_row == asked).astype(BF16)
    finish(precv_ref, groups - 1, hr_sem)
    taken = unblocks(precv_ref[...])
    for which in range(2):
        dense = dot(pput_ref[which], taken[:, which * quarter:(which + 1) * quarter])
        bsend_ref[which] = dense.reshape(nd, rows // nd, quarter).astype(BF16)
    homes = [x_at * nz + ahead(z_at, k_at, nz), x_at * nz + ahead(z_at, jnp.where(k_at > 0, nz - k_at, 0), nz)]

    def home(which, peer):
        return pltpu.make_async_remote_copy(
            src_ref=bsend_ref.at[which, peer], dst_ref=brecv_ref.at[which, z_at],
            send_sem=bs_sem.at[which], recv_sem=br_sem.at[which],
            device_id={"dp": peer, "emb": homes[which]}, device_id_type=MESH,
        )

    for peer in dp_peers:
        for which in range(2):
            home(which, peer).start()

    @pl.when(k_at > 0)
    def _():
        for which in range(2):
            home(which, dp).start()

    @pl.when(k_at == 0)
    def _():
        for which in range(2):
            pltpu.make_async_copy(
                bsend_ref.at[which, dp], brecv_ref.at[which, z_at], br_sem.at[which]
            ).start()

    finish(grecv_ref, groups - 1, gr_sem)
    dense = dot(put_ref[...], unblocks(grecv_ref[...]))
    dsend_ref[...] = dense.reshape(nd, rows // nd, part).astype(BF16)
    for peer in dp_peers:
        pltpu.make_async_remote_copy(
            src_ref=dsend_ref.at[peer], dst_ref=drecv_ref.at[dp], send_sem=ds_sem, recv_sem=dr_sem,
            device_id={"dp": peer}, device_id_type=MESH,
        ).start()
    drecv_ref[dp] = dsend_ref[dp]

    finish(drecv_ref, nd - 1, dr_sem)
    out_ref[:, :part] = jnp.sum(drecv_ref[...].astype(F32), axis=0)
    for which in range(2):
        finish(brecv_ref.at[which], nz, br_sem.at[which])
        cols = slice(part + which * quarter, part + (which + 1) * quarter)
        out_ref[:, cols] = jnp.sum(brecv_ref[which].astype(F32), axis=0)

    finish(ask_ref, nz - 1, zs_sem)
    finish(comb_ref, nx - 1, xs_sem)
    finish(pask_ref, nd - 1, ps_sem)
    finish(pcomb_ref, nx - 1, qs_sem)
    finish(send_ref, groups - 1, rs_sem)
    finish(gsend_ref, groups - 1, gs_sem)
    finish(psend_ref, groups - 1, hs_sem)
    finish(dsend_ref, nd - 1, ds_sem)
    for which in range(2):
        finish(bsend_ref.at[which], nd - 1, bs_sem.at[which])

    @pl.when(k_at > 0)
    def _():
        for which in range(2):
            finish(bsend_ref.at[which], 1, bs_sem.at[which])


def layer(nx, nz, nd, table, item_shard, item_row, segment_ids, grad_out, w_in, w_out):
    tokens, width = grad_out.shape
    rows = table.shape[0]
    groups = nx * nz
    lanes = nz * CAP
    part = width // 2
    quarter = part // 2
    vmem = pl.BlockSpec(memory_space=pltpu.VMEM)
    anywhere = pl.BlockSpec(memory_space=pl.ANY)
    dma = pltpu.SemaphoreType.DMA
    pairs = HEADS // 2
    return pl.pallas_call(
        functools.partial(kernel, nx, nz, nd),
        out_shape=(
            pltpu.VMEM((tokens, width), BF16),
            pltpu.VMEM((rows // nd, width), F32),
        ),
        in_specs=[anywhere] * 7,
        out_specs=(vmem, vmem),
        scratch_shapes=[
            pltpu.VMEM((1, tokens), jnp.int32),
            pltpu.VMEM((1, tokens), jnp.int32),
            pltpu.VMEM((1, tokens), jnp.int32),
            pltpu.VMEM((rows, width), BF16),
            pltpu.VMEM((tokens, width), BF16),
            pltpu.VMEM((width, 4 * width), BF16),
            pltpu.VMEM((width, width), BF16),
            pltpu.VMEM((nz, nx, lanes), F32),
            pltpu.VMEM((nz, nx, lanes), F32),
            pltpu.VMEM((nx, 1, lanes), F32),
            pltpu.VMEM((nx, 1, lanes), F32),
            pltpu.VMEM((nz, 2 * nx, lanes), F32),
            pltpu.VMEM((nd, 2 * nx, lanes), F32),
            pltpu.VMEM((nx, 2, lanes), F32),
            pltpu.VMEM((nx, 2, lanes), F32),
            pltpu.VMEM((tokens, groups * CAP), BF16),
            pltpu.VMEM((groups * CAP, tokens), BF16),
            pltpu.VMEM((2, groups * CAP, tokens), BF16),
            pltpu.VMEM((rows, groups * CAP), BF16),
            pltpu.VMEM((2, rows, groups * CAP), BF16),
            pltpu.VMEM((groups, 2 * CAP, width // 2), BF16),
            pltpu.VMEM((groups, 2 * CAP, width // 2), BF16),
            pltpu.VMEM((tokens, width), BF16),
            pltpu.VMEM((tokens, width), BF16),
            pltpu.VMEM((tokens, tokens), F32),
            pltpu.VMEM((tokens, width), BF16),
            pltpu.VMEM((4 * width, width), BF16),
            pltpu.VMEM((tokens, 4 * width), BF16),
            pltpu.VMEM((tokens, 4 * width), F32),
            pltpu.VMEM((pairs, 2 * tokens, tokens), BF16),
            pltpu.VMEM((pairs, 2 * tokens, tokens), F32),
            pltpu.VMEM((tokens, 4 * width), BF16),
            pltpu.VMEM((groups, 2 * CAP, quarter), BF16),
            pltpu.VMEM((groups, 2 * CAP, quarter), BF16),
            pltpu.VMEM((groups, 2 * CAP, quarter), BF16),
            pltpu.VMEM((groups, 2 * CAP, quarter), BF16),
            pltpu.VMEM((nd, rows // nd, part), BF16),
            pltpu.VMEM((nd, rows // nd, part), BF16),
            pltpu.VMEM((2, nd, rows // nd, quarter), BF16),
            pltpu.VMEM((2, nz, rows // nd, quarter), BF16),
            dma((7,)),
        ]
        + [dma] * 16
        + [dma((2,))] * 2,
        compiler_params=pltpu.CompilerParams(
            collective_id=0, has_side_effects=True, vmem_limit_bytes=60 * 2**20
        ),
        name="hstu",
    )(item_shard.reshape(1, tokens), item_row.reshape(1, tokens), segment_ids, table, grad_out, w_in, w_out)


def solution(mesh, nx=4):
    return jax.shard_map(
        functools.partial(layer, nx, mesh.shape["emb"] // nx, mesh.shape["dp"]),
        mesh=mesh,
        in_specs=(
            P("emb", None),
            P(("dp", "emb"), None),
            P(("dp", "emb")),
            P(("dp", "emb"), None),
            P(("dp", "emb"), None),
            P(),
            P(),
        ),
        out_specs=(P(("dp", "emb"), None), P(("emb", "dp"), None)),
        check_vma=False,
    )
```

```python
import functools

import jax
import jax.numpy as jnp
from jax import lax
from jax.experimental import pallas as pl
from jax.experimental.pallas import tpu as pltpu
from jax.sharding import PartitionSpec as P

HEADS = 8
CAP = 8
MOST = 128
MESH = pl.DeviceIdType.MESH
F32 = jnp.float32
BF16 = jnp.bfloat16


def dot(a, b, contract=(1, 0)):
    return lax.dot_general(
        a, b, (((contract[0],), (contract[1],)), ((), ())), preferred_element_type=F32
    )


def iota(shape, axis):
    return lax.broadcasted_iota(jnp.int32, shape, axis)


def to_col(row):
    n = row.shape[1]
    return jnp.sum(jnp.where(iota((n, n), 0) == iota((n, n), 1), row, 0.0), axis=1, keepdims=True)


def sigmoid(value):
    return 0.5 * jnp.tanh(0.5 * value) + 0.5


def ahead(at, distance, size):
    to = at + distance
    return jnp.where(to >= size, to - size, to)


def around(at, size, act):
    act(ahead(at, size // 2, size))

    def both(step, carry):
        distance = size // 2 - 1 - step
        act(ahead(at, distance, size))
        act(ahead(at, size - distance, size))
        return carry

    lax.fori_loop(0, size // 2 - 1, both, 0)


def forward_backward(factor_ref, d_gated_ref, x_ref, win_ref, gated_ref,
                     proj_ref, slope_ref, weight_ref, wslope_ref, dz_ref):
    tokens, width = x_ref.shape
    pairs = HEADS // 2
    lanes = 2 * width // HEADS
    scale = (width // HEADS) ** -0.5

    def part(index):
        return slice(index * width, (index + 1) * width)

    x = x_ref[...]
    for index in range(4):
        z = dot(x, win_ref[:, part(index)])
        sig = sigmoid(z)
        act = z * sig
        proj_ref[:, part(index)] = act.astype(BF16)
        slope_ref[:, part(index)] = sig + act * (1.0 - sig)

    middle = tokens // 2
    spans = [(slice(0, middle), middle, slice(tokens, 2 * tokens)), (slice(middle, tokens), tokens, slice(0, tokens))]
    first = iota((middle, lanes), 1) < lanes // 2

    def stack(value):
        zero = jnp.zeros_like(value)
        return jnp.concatenate([jnp.where(first, value, zero), jnp.where(first, zero, value)], axis=0)

    def unstack(value):
        return jnp.where(first, value[:middle], value[middle:])

    def pair(index, which):
        start = which * width + index * lanes
        return slice(start, start + lanes)

    attended = []
    for index in range(pairs):
        seen = []
        for span, keys, at in spans:
            q = stack(proj_ref[span, pair(index, 2)])
            s = dot(q, proj_ref[:keys, pair(index, 3)], (1, 1)) * scale
            sig = sigmoid(s)
            act = s * sig
            factor = factor_ref[span, :keys]
            factor = jnp.concatenate([factor, factor], axis=0)
            weights = (act * factor).astype(BF16)
            weight_ref[index, at, :keys] = weights
            wslope_ref[index, at, :keys] = (sig + act * (1.0 - sig)) * (factor * scale)
            seen.append(unstack(dot(weights, proj_ref[:keys, pair(index, 1)])))
        attended.append(jnp.concatenate(seen, axis=0))
    attended = jnp.concatenate(attended, axis=1)

    center = attended - jnp.mean(attended, axis=1, keepdims=True)
    rstd = lax.rsqrt(jnp.mean(center * center, axis=1, keepdims=True) + 1e-05)
    normed = center * rstd
    u = proj_ref[:, part(0)].astype(F32)
    gated_ref[...] = (normed * u).astype(BF16)

    d_gated = d_gated_ref[...].astype(F32)
    d_u = (d_gated * normed).astype(BF16).astype(F32)
    dz_ref[:, part(0)] = (d_u * slope_ref[:, part(0)]).astype(BF16)
    d_normed = d_gated * u
    d_att = rstd * (
        d_normed
        - jnp.mean(d_normed, axis=1, keepdims=True)
        - normed * jnp.mean(d_normed * normed, axis=1, keepdims=True)
    )
    d_att = d_att.astype(BF16)

    def put(index, which, value):
        value = value.astype(BF16).astype(F32)
        dz_ref[:, pair(index, which)] = (value * slope_ref[:, pair(index, which)]).astype(BF16)

    def whole(early, late):
        return jnp.concatenate([early + late[:middle], late[middle:]], axis=0)

    for index in range(pairs):
        d_v, d_q, d_k = [], [], []
        for span, keys, at in spans:
            q = stack(proj_ref[span, pair(index, 2)])
            d = stack(d_att[span, index * lanes:(index + 1) * lanes])
            d_v.append(dot(weight_ref[index, at, :keys], d, (0, 0)))
            d_s = dot(d, proj_ref[:keys, pair(index, 1)], (1, 1)) * wslope_ref[index, at, :keys]
            d_s = d_s.astype(BF16)
            d_q.append(unstack(dot(d_s, proj_ref[:keys, pair(index, 3)])))
            d_k.append(dot(d_s, q, (0, 0)))
        put(index, 1, whole(*d_v))
        put(index, 2, jnp.concatenate(d_q, axis=0))
        put(index, 3, whole(*d_k))


def kernel(nx, nz, nd,
           owner_hbm, row_hbm, seg_hbm, table_hbm, grad_hbm, win_hbm, wout_hbm,
           mixed_ref, out_ref,
           owner_ref, row_ref, seg_ref, table_ref, grad_ref, win_ref, wout_ref,
           ask_ref, mid_ref, comb_ref, fin_ref, pask_ref, pmid_ref, pcomb_ref, pfin_ref,
           place_ref, back_ref, pback_ref, put_ref, pput_ref,
           send_ref, recv_ref, x_ref, gated_ref, factor_ref, d_gated_ref, wint_ref,
           proj_ref, slope_ref, weight_ref, wslope_ref, dz_ref,
           gsend_ref, grecv_ref, psend_ref, precv_ref, dsend_ref, drecv_ref, bsend_ref, brecv_ref,
           load_sem, zs_sem, zr_sem, xs_sem, xr_sem, ps_sem, pr_sem, qs_sem, qr_sem, rs_sem, rr_sem,
           gs_sem, gr_sem, hs_sem, hr_sem, ds_sem, dr_sem, bs_sem, br_sem):
    emb = lax.axis_index("emb")
    dp = lax.axis_index("dp")
    x_at, z_at = emb // nz, emb % nz
    groups = nx * nz
    tokens, width = x_ref.shape
    rows = table_ref.shape[0]
    lanes = nz * CAP

    loads = [
        pltpu.make_async_copy(source, target, load_sem.at[index])
        for index, (source, target) in enumerate(
            [(owner_hbm, owner_ref), (row_hbm, row_ref), (seg_hbm, seg_ref), (table_hbm, table_ref),
             (win_hbm, win_ref), (wout_hbm, wout_ref), (grad_hbm, grad_ref)]
        )
    ]
    for load in loads[:2]:
        load.start()

    barrier = pltpu.get_barrier_semaphore()

    def greet(peer, axis):
        pl.semaphore_signal(barrier, 1, device_id={axis: peer}, device_id_type=MESH)

    ny = nd // 2
    far = [way for step in range(ny // 2, 0, -1) for way in ((step, ny - step) if 2 * step < ny else (step,))]
    y_at, core_at = dp // 2, dp % 2
    k_at = y_at + ny * core_at
    plane = [(ahead(y_at, way, ny), core) for way in far for core in range(2)] + [(y_at, 1 - core_at)]
    plane = [(y * 2 + core, y + ny * core) for y, core in plane]
    dp_peers = [peer for peer, _ in plane]
    x_all = [ahead(x_at, step, nx) for step in range(nx)]

    around(z_at, nz, lambda to: greet(x_at * nz + to, "emb"))
    for to in x_all[1:]:
        greet(to * nz + z_at, "emb")
    for peer in dp_peers:
        greet(peer, "dp")
    for load in loads[2:]:
        load.start()

    def finish(ref, count, sem):
        pltpu.make_async_copy(ref.at[pl.ds(0, count)], ref.at[pl.ds(0, count)], sem).wait()

    loads[0].wait()
    owner = owner_ref[...].astype(F32)
    named = iota((groups, tokens), 0).astype(F32) == owner
    before = (iota((tokens, tokens), 0) < iota((tokens, tokens), 1)).astype(BF16)
    named_bf = named.astype(BF16)
    slot = jnp.sum(jnp.where(named, dot(named_bf, before), 0.0), axis=0, keepdims=True)
    target = owner * CAP + slot
    loads[1].wait()
    number = to_col((row_ref[...] + 1).astype(F32))
    slot_col = to_col(slot)
    lane_at = iota((tokens, lanes), 1).astype(F32)
    here = slot_col + (z_at * CAP).astype(F32) == lane_at
    high = jnp.floor(number * (1.0 / 16.0))
    low = number - 16.0 * high

    def numbers(named_bf, here):
        return 16.0 * dot(named_bf, jnp.where(here, high, 0.0).astype(BF16)) + dot(
            named_bf, jnp.where(here, low, 0.0).astype(BF16)
        )

    ask = numbers(named_bf, here)
    for at in range(nx):
        ask_ref[:, pl.ds(at, 1), :] = ask[at * nz:(at + 1) * nz].reshape(nz, 1, lanes)

    pl.semaphore_wait(barrier, nz + nx + nd - 3)

    def ask_z(peer):
        pltpu.make_async_remote_copy(
            src_ref=ask_ref.at[peer], dst_ref=mid_ref.at[z_at], send_sem=zs_sem, recv_sem=zr_sem,
            device_id={"emb": x_at * nz + peer}, device_id_type=MESH,
        ).start()

    around(z_at, nz, ask_z)
    mid_ref[z_at] = ask_ref[z_at]

    finish(mid_ref, nz - 1, zr_sem)
    comb = jnp.sum(mid_ref[...], axis=0)
    for at in range(nx):
        comb_ref[at] = comb[at:at + 1]

    for peer in x_all[1:]:
        pltpu.make_async_remote_copy(
            src_ref=comb_ref.at[peer], dst_ref=fin_ref.at[x_at], send_sem=xs_sem, recv_sem=xr_sem,
            device_id={"emb": peer * nz + z_at}, device_id_type=MESH,
        ).start()
    fin_ref[x_at] = comb_ref[x_at]

    def send_all(places, source, target, send_sem, recv_sem):
        def send(peer):
            pltpu.make_async_remote_copy(
                src_ref=source.at[peer], dst_ref=target.at[emb], send_sem=send_sem, recv_sem=recv_sem,
                device_id={"emb": peer}, device_id_type=MESH,
            ).start()

        def send_z(to):
            for at in places:
                send(at * nz + to)

        around(z_at, nz, send_z)
        for at in places:
            if at is not x_all[0]:
                send(at * nz + z_at)

    def blocks(value):
        half = value.shape[1] // 2
        left = value[:, :half].reshape(nz, CAP, half)
        right = value[:, half:].reshape(nz, CAP, half)
        return jnp.concatenate([left, right], axis=1).astype(BF16)

    def together(value):
        return jnp.concatenate([blocks(value[at * lanes:(at + 1) * lanes]) for at in range(nx)], axis=0)

    def unblocks(value):
        half = value.shape[2]
        value = value.astype(F32)
        left = value[:, :CAP].reshape(groups * CAP, half)
        right = value[:, CAP:].reshape(groups * CAP, half)
        return jnp.concatenate([left, right], axis=1).astype(BF16)

    loads[3].wait()

    def answer(at):
        asked = to_col(fin_ref[at])
        pick = (asked == (iota((lanes, rows), 1) + 1).astype(F32)).astype(BF16)
        send_ref[pl.ds(at * nz, nz)] = blocks(dot(pick, table_ref[...]))

    answer(x_at)
    send_all(x_all[:1], send_ref, recv_ref, rs_sem, rr_sem)
    finish(fin_ref, nx - 1, xr_sem)
    for at in x_all[1:]:
        answer(at)
    send_all(x_all[1:], send_ref, recv_ref, rs_sem, rr_sem)
    recv_ref[emb] = send_ref[emb]

    owner_x = jnp.floor(owner * (1.0 / nz))
    ahead_z = owner - nz * owner_x - z_at.astype(F32)
    ahead_z = jnp.where(ahead_z < 0.0, ahead_z + nz, ahead_z)
    behind_z = jnp.where(ahead_z > 0.0, nz - ahead_z, 0.0)
    served = [owner_x * nz + ahead_z, owner_x * nz + behind_z]
    here = slot_col + (dp * CAP).astype(F32) == lane_at
    device = iota((groups, tokens), 0).astype(F32)
    pask = numbers(jnp.concatenate([device == one for one in served], axis=0).astype(BF16), here)
    for at in range(2 * nx):
        pask_ref[:, pl.ds(at, 1), :] = pask[at % 2 * groups + at // 2 * nz:][:nz].reshape(nz, 1, lanes)
    for peer, k in plane:
        pltpu.make_async_remote_copy(
            src_ref=pask_ref.at[k], dst_ref=pmid_ref.at[dp], send_sem=ps_sem, recv_sem=pr_sem,
            device_id={"dp": peer}, device_id_type=MESH,
        ).start()
    pmid_ref[dp] = pask_ref[k_at]

    place_ref[...] = (to_col(target) == iota((tokens, groups * CAP), 1).astype(F32)).astype(BF16)
    at_slot = iota((groups * CAP, tokens), 0).astype(F32)
    back_ref[...] = (at_slot == target).astype(BF16)
    for which in range(2):
        pback_ref[which] = (at_slot == served[which] * CAP + slot).astype(BF16)
    at_row = (iota((rows, groups * CAP), 0) + 1).astype(F32)
    put_ref[...] = (at_row == jnp.concatenate([fin_ref[at] for at in range(nx)], axis=1)).astype(BF16)
    for index in (2, 4, 5, 6):
        loads[index].wait()
    seg_row = seg_ref[...].astype(F32)
    seen = (iota((tokens, tokens), 1) <= iota((tokens, tokens), 0)) & (to_col(seg_row) == seg_row)
    factor_ref[...] = jnp.where(seen, 1.0 / MOST, 0.0)
    wint_ref[...] = win_ref[...].T
    d_gated_ref[...] = dot(grad_ref[...], wout_ref[...], (1, 1)).astype(BF16)

    finish(recv_ref, groups - 1, rr_sem)
    x_ref[...] = dot(place_ref[...], unblocks(recv_ref[...])).astype(BF16)

    forward_backward(factor_ref, d_gated_ref, x_ref, win_ref, gated_ref,
                     proj_ref, slope_ref, weight_ref, wslope_ref, dz_ref)

    finish(pmid_ref, nd - 1, pr_sem)
    pcomb = jnp.sum(pmid_ref[...], axis=0)
    for at in range(nx):
        pcomb_ref[at] = pcomb[2 * at:2 * at + 2]
    for peer in x_all[1:]:
        pltpu.make_async_remote_copy(
            src_ref=pcomb_ref.at[peer], dst_ref=pfin_ref.at[x_at], send_sem=qs_sem, recv_sem=qr_sem,
            device_id={"emb": peer * nz + z_at}, device_id_type=MESH,
        ).start()
    pfin_ref[x_at] = pcomb_ref[x_at]

    part = width // 2
    quarter = part // 2

    def d_x(cols):
        value = dot(dz_ref[...], wint_ref[:, cols]).astype(BF16).astype(F32)
        return (value + grad_ref[:, cols].astype(F32)).astype(BF16)

    gsend_ref[...] = together(dot(back_ref[...], d_x(slice(0, part))))
    send_all(x_all, gsend_ref, grecv_ref, gs_sem, gr_sem)
    grecv_ref[emb] = gsend_ref[emb]

    right = d_x(slice(part, width))
    given = [dot(pback_ref[which], right[:, which * quarter:(which + 1) * quarter]) for which in range(2)]
    psend_ref[...] = together(jnp.concatenate(given, axis=1))
    for peer, k in plane + [(dp, k_at)]:
        for at in x_all:
            if peer is dp and at is x_all[0]:
                continue
            pltpu.make_async_remote_copy(
                src_ref=psend_ref.at[at * nz + k], dst_ref=precv_ref.at[x_at * nd + dp],
                send_sem=hs_sem, recv_sem=hr_sem,
                device_id={"dp": peer, "emb": at * nz + z_at}, device_id_type=MESH,
            ).start()
    precv_ref[x_at * nd + dp] = psend_ref[x_at * nz + k_at]

    mixed_ref[...] = (dot(gated_ref[...], wout_ref[...]) + x_ref[...].astype(F32)).astype(BF16)

    finish(pfin_ref, nx - 1, qr_sem)
    at_row = (iota((rows, groups * CAP), 0) + 1).astype(F32)
    for which in range(2):
        asked = jnp.concatenate([pfin_ref[at][which:which + 1] for at in range(nx)], axis=1)
        pput_ref[which] = (at_row == asked).astype(BF16)
    finish(precv_ref, groups - 1, hr_sem)
    taken = unblocks(precv_ref[...])
    for which in range(2):
        dense = dot(pput_ref[which], taken[:, which * quarter:(which + 1) * quarter])
        bsend_ref[which] = dense.reshape(nd, rows // nd, quarter).astype(BF16)
    homes = [x_at * nz + ahead(z_at, k_at, nz), x_at * nz + ahead(z_at, jnp.where(k_at > 0, nz - k_at, 0), nz)]

    def home(which, peer):
        return pltpu.make_async_remote_copy(
            src_ref=bsend_ref.at[which, peer], dst_ref=brecv_ref.at[which, z_at],
            send_sem=bs_sem.at[which], recv_sem=br_sem.at[which],
            device_id={"dp": peer, "emb": homes[which]}, device_id_type=MESH,
        )

    for peer in dp_peers:
        for which in range(2):
            home(which, peer).start()

    @pl.when(k_at > 0)
    def _():
        for which in range(2):
            home(which, dp).start()

    @pl.when(k_at == 0)
    def _():
        for which in range(2):
            pltpu.make_async_copy(
                bsend_ref.at[which, dp], brecv_ref.at[which, z_at], br_sem.at[which]
            ).start()

    finish(grecv_ref, groups - 1, gr_sem)
    dense = dot(put_ref[...], unblocks(grecv_ref[...]))
    dsend_ref[...] = dense.reshape(nd, rows // nd, part).astype(BF16)
    for peer in dp_peers:
        pltpu.make_async_remote_copy(
            src_ref=dsend_ref.at[peer], dst_ref=drecv_ref.at[dp], send_sem=ds_sem, recv_sem=dr_sem,
            device_id={"dp": peer}, device_id_type=MESH,
        ).start()
    drecv_ref[dp] = dsend_ref[dp]

    finish(drecv_ref, nd - 1, dr_sem)
    out_ref[:, :part] = jnp.sum(drecv_ref[...].astype(F32), axis=0)
    for which in range(2):
        finish(brecv_ref.at[which], nz, br_sem.at[which])
        cols = slice(part + which * quarter, part + (which + 1) * quarter)
        out_ref[:, cols] = jnp.sum(brecv_ref[which].astype(F32), axis=0)

    finish(ask_ref, nz - 1, zs_sem)
    finish(comb_ref, nx - 1, xs_sem)
    finish(pask_ref, nd - 1, ps_sem)
    finish(pcomb_ref, nx - 1, qs_sem)
    finish(send_ref, groups - 1, rs_sem)
    finish(gsend_ref, groups - 1, gs_sem)
    finish(psend_ref, groups - 1, hs_sem)
    finish(dsend_ref, nd - 1, ds_sem)
    for which in range(2):
        finish(bsend_ref.at[which], nd - 1, bs_sem.at[which])

    @pl.when(k_at > 0)
    def _():
        for which in range(2):
            finish(bsend_ref.at[which], 1, bs_sem.at[which])


def layer(nx, nz, nd, table, item_shard, item_row, segment_ids, grad_out, w_in, w_out):
    tokens, width = grad_out.shape
    rows = table.shape[0]
    groups = nx * nz
    lanes = nz * CAP
    part = width // 2
    quarter = part // 2
    vmem = pl.BlockSpec(memory_space=pltpu.VMEM)
    anywhere = pl.BlockSpec(memory_space=pl.ANY)
    dma = pltpu.SemaphoreType.DMA
    pairs = HEADS // 2
    return pl.pallas_call(
        functools.partial(kernel, nx, nz, nd),
        out_shape=(
            pltpu.VMEM((tokens, width), BF16),
            pltpu.VMEM((rows // nd, width), F32),
        ),
        in_specs=[anywhere] * 7,
        out_specs=(vmem, vmem),
        scratch_shapes=[
            pltpu.VMEM((1, tokens), jnp.int32),
            pltpu.VMEM((1, tokens), jnp.int32),
            pltpu.VMEM((1, tokens), jnp.int32),
            pltpu.VMEM((rows, width), BF16),
            pltpu.VMEM((tokens, width), BF16),
            pltpu.VMEM((width, 4 * width), BF16),
            pltpu.VMEM((width, width), BF16),
            pltpu.VMEM((nz, nx, lanes), F32),
            pltpu.VMEM((nz, nx, lanes), F32),
            pltpu.VMEM((nx, 1, lanes), F32),
            pltpu.VMEM((nx, 1, lanes), F32),
            pltpu.VMEM((nz, 2 * nx, lanes), F32),
            pltpu.VMEM((nd, 2 * nx, lanes), F32),
            pltpu.VMEM((nx, 2, lanes), F32),
            pltpu.VMEM((nx, 2, lanes), F32),
            pltpu.VMEM((tokens, groups * CAP), BF16),
            pltpu.VMEM((groups * CAP, tokens), BF16),
            pltpu.VMEM((2, groups * CAP, tokens), BF16),
            pltpu.VMEM((rows, groups * CAP), BF16),
            pltpu.VMEM((2, rows, groups * CAP), BF16),
            pltpu.VMEM((groups, 2 * CAP, width // 2), BF16),
            pltpu.VMEM((groups, 2 * CAP, width // 2), BF16),
            pltpu.VMEM((tokens, width), BF16),
            pltpu.VMEM((tokens, width), BF16),
            pltpu.VMEM((tokens, tokens), F32),
            pltpu.VMEM((tokens, width), BF16),
            pltpu.VMEM((4 * width, width), BF16),
            pltpu.VMEM((tokens, 4 * width), BF16),
            pltpu.VMEM((tokens, 4 * width), F32),
            pltpu.VMEM((pairs, 2 * tokens, tokens), BF16),
            pltpu.VMEM((pairs, 2 * tokens, tokens), F32),
            pltpu.VMEM((tokens, 4 * width), BF16),
            pltpu.VMEM((groups, 2 * CAP, quarter), BF16),
            pltpu.VMEM((groups, 2 * CAP, quarter), BF16),
            pltpu.VMEM((groups, 2 * CAP, quarter), BF16),
            pltpu.VMEM((groups, 2 * CAP, quarter), BF16),
            pltpu.VMEM((nd, rows // nd, part), BF16),
            pltpu.VMEM((nd, rows // nd, part), BF16),
            pltpu.VMEM((2, nd, rows // nd, quarter), BF16),
            pltpu.VMEM((2, nz, rows // nd, quarter), BF16),
            dma((7,)),
        ]
        + [dma] * 16
        + [dma((2,))] * 2,
        compiler_params=pltpu.CompilerParams(
            collective_id=0, has_side_effects=True, vmem_limit_bytes=60 * 2**20
        ),
        name="hstu",
    )(item_shard.reshape(1, tokens), item_row.reshape(1, tokens), segment_ids, table, grad_out, w_in, w_out)


def solution(mesh, nx=4):
    return jax.shard_map(
        functools.partial(layer, nx, mesh.shape["emb"] // nx, mesh.shape["dp"]),
        mesh=mesh,
        in_specs=(
            P("emb", None),
            P(("dp", "emb"), None),
            P(("dp", "emb")),
            P(("dp", "emb"), None),
            P(("dp", "emb"), None),
            P(),
            P(),
        ),
        out_specs=(P(("dp", "emb"), None), P(("emb", "dp"), None)),
        check_vma=False,
    )
```
